128 devices in a mesh: rows: 32 (over x, y, core), grp: 4 (over z).
Axes of the slice: x: 4, y: 4, z: 4, core: 2. Of those that a mesh axis runs over, the one named last changes fastest.
Arguments:
- embeddings: bfloat16 [131072, 768], P('rows')
- partner: int32 [32, 32], P(None, 'rows'), may hold values from 0 to 15
- links: int32 [32, 32, 4], P('rows'), may hold values from 0 to 15, as said below
- counts: int32 [32, 32], P('rows'), may hold values from 0 to 4, as said below
Outputs:
- refined: bfloat16 [131072, 768], P('rows')
The draws below stay inside these ranges and needn't reach their ends.
Inputs may be any that keep to these rules, and one draw needn't show every extreme that they name: The 4 entries of links[d, p] are different local block numbers. counts[d, d] is 0; 0 means that rows index d pairs none of its blocks with rows index p.
All inputs are finite; a program needn't handle non-finite values.
Results may differ from the reference program's by a relative error of at most 0.0038.
Values may be sent and summed in bfloat16 or wider, within the bound.
A program may use at most 192 MiB of HBM per device.

```python
import math
import jax
import jax.numpy as jnp
from jax import lax

D = 768
BLOCK = 256
BLK_DEV = 16
LINKS = 4
ROUNDS = 1
NB = 512
ROWS_ALL = 131072
N_ROWS = 32


def draw_embeddings(key, part):
    key_centre, key_topic, key_noise, key_scale, key_common, key_share = jax.random.split(key, 6)
    topic_total = 4 * BLOCK
    centres = jax.random.normal(key_centre, (topic_total, D), jnp.float32)
    topics = jax.random.randint(key_topic, (ROWS_ALL,), 0, topic_total)
    common = jax.random.normal(key_common, (1, D), jnp.float32)
    noise = jax.random.normal(key_noise, (ROWS_ALL, D), jnp.float32)
    strength = 0.9
    scales = jnp.exp(jax.random.uniform(key_scale, (ROWS_ALL, 1), jnp.float32, 0.0, math.log(10.0)))
    shares = jax.random.uniform(key_share, (ROWS_ALL, 1), jnp.float32, 0.0, 0.6)
    topical = strength * centres[topics] + math.sqrt(1.0 - strength * strength) * noise
    mixed = shares * common + jnp.sqrt(1.0 - shares * shares) * topical
    return (mixed * scales).astype(jnp.bfloat16)


def draw_links(key, part):
    scores = jax.random.randint(key, (N_ROWS, N_ROWS, BLK_DEV), 0, 1 << 20) * BLK_DEV
    scores = scores + jnp.arange(BLK_DEV, dtype=jnp.int32)
    ranked = jnp.argsort(scores, axis=-1)
    return ranked[..., :LINKS].astype(jnp.int32)


def draw_counts(key, part):
    key_roll, key_size = jax.random.split(key, 2)
    offsets = (jnp.arange(N_ROWS, dtype=jnp.int32)[None, :] - jnp.arange(N_ROWS, dtype=jnp.int32)[:, None]) % N_ROWS
    reach = jnp.minimum(offsets, N_ROWS - offsets)
    roll = jax.random.randint(key_roll, (N_ROWS, N_ROWS), 0, N_ROWS)
    listed = (roll >= 2 * reach - 2) & (offsets != 0)
    sizes_drawn = jax.random.randint(key_size, (N_ROWS, N_ROWS), 1, LINKS + 1)
    sizes_drawn = jnp.where(offsets == 1, LINKS, sizes_drawn)
    return jnp.where(listed, sizes_drawn, 0).astype(jnp.int32)


def set_ends(array, key, least, largest):
    dims = array.shape
    spot = [jax.random.randint(jax.random.fold_in(key, axis), (), 0, dims[axis]) for axis in range(len(dims))]
    array = array.at[tuple(spot)].set(least)
    longest = dims.index(max(dims))
    spot[longest] = (spot[longest] + 1) % dims[longest]
    return array.at[tuple(spot)].set(largest)


def setup_inputs(seed: int = 0) -> dict:
    key_of = jax.random.split(jax.random.key(seed), 5)
    return {
        "embeddings": draw_embeddings(jax.random.fold_in(key_of[4], 71), 0),
        "partner": set_ends(jax.random.randint(key_of[1], (N_ROWS, N_ROWS), 0, BLK_DEV), jax.random.fold_in(key_of[1], 1), 0, BLK_DEV - 1).astype(jnp.int32),
        "links": draw_links(jax.random.fold_in(key_of[4], 71), 0),
        "counts": draw_counts(jax.random.fold_in(key_of[4], 71), 0),
    }


def row_scaled(values):
    return values * lax.rsqrt(lax.optimization_barrier(jnp.mean(values * values, axis=-1, keepdims=True)) + 1e-06)

def diagonal_term(block):
    features = block.shape[-1]
    cosines = jnp.dot(block, block.T, preferred_element_type=jnp.float32) / features
    weight = (jnp.maximum(cosines, 0.0) ** 3).astype(jnp.bfloat16)
    return jnp.dot(weight, block, preferred_element_type=jnp.float32)

def reference(embeddings, partner, links, counts):
    features = embeddings.shape[1]
    current = embeddings
    for round_index in range(ROUNDS):
        normed = row_scaled(current.astype(jnp.float32)).astype(jnp.bfloat16)
        blocks = normed.reshape(N_ROWS, BLK_DEV, BLOCK, features)
        totals = lax.map(diagonal_term, normed.reshape(NB, BLOCK, features))
        totals = totals.reshape(N_ROWS, BLK_DEV, BLOCK, features)

        def visit(position, totals):
            device = position // N_ROWS
            peer = position % N_ROWS
            remote_index = partner[device, peer]
            remote = blocks[peer, remote_index]
            picked = links[device, peer]
            own_blocks = blocks[device][picked]
            cosines = jnp.einsum('kad,bd->kab', own_blocks.astype(jnp.float32), remote.astype(jnp.float32)) / features
            active = (jnp.arange(LINKS) < counts[device, peer])[:, None, None]
            weight = jnp.where(active, jnp.maximum(cosines, 0.0) ** 3, 0.0).astype(jnp.bfloat16)
            forward = jnp.einsum('kab,bd->kad', weight.astype(jnp.float32), remote.astype(jnp.float32))
            totals = totals.at[device, picked].add(forward)
            returned_term = jnp.einsum('kab,kad->bd', weight.astype(jnp.float32), own_blocks.astype(jnp.float32)).astype(jnp.bfloat16)
            totals = totals.at[peer, remote_index].add(returned_term.astype(jnp.float32))
            return totals
        totals = lax.fori_loop(0, N_ROWS * N_ROWS, visit, totals)
        current = row_scaled(totals).astype(jnp.bfloat16).reshape(ROWS_ALL, features)
    return current
```

```python
import functools

import jax
import jax.numpy as jnp
from jax import lax
from jax.experimental import pallas as pl
from jax.experimental.pallas import tpu as pltpu
from jax.sharding import PartitionSpec as P

BLOCK = 256
FEATURES = 768
BLK_DEV = 16
LINKS = 4
GROUPS = 4
SLOTS = 8
CHUNKS = 4
CHUNK_ROWS = BLOCK // CHUNKS
PIECE = 16
MESH = pl.DeviceIdType.MESH


def peer_at(me, group, slot, sign):
    step_x = slot // 2
    step_y = step_x + group
    flip = slot % 2
    x, y, core = me // 8, (me // 2) % 4, me % 2
    return ((x + sign * step_x + 8) % 4) * 8 + ((y + sign * step_y + 8) % 4) * 2 + (core + flip) % 2


def is_remote(group, slot):
    return jnp.logical_or(group != 0, slot != 0)


def row_scaled(values):
    return values * lax.rsqrt(jnp.mean(values * values, axis=-1, keepdims=True) + 1e-06)


def fetch_kernel(wanted, emb, normed, fetched, raw, nb, out, in_sem, norm_sem, send_sem, recv_sem):
    me = lax.axis_index("rows")
    group = lax.axis_index("grp")

    for b in range(BLK_DEV):
        pltpu.make_async_copy(emb.at[b], raw.at[b], in_sem.at[b]).start()

    barrier = pltpu.get_barrier_semaphore()

    def greet(slot, carry):
        @pl.when(is_remote(group, slot))
        def _():
            pl.semaphore_signal(
                barrier, inc=1, device_id={"rows": peer_at(me, group, slot, -1)}, device_id_type=MESH
            )

        return carry

    lax.fori_loop(0, SLOTS, greet, 0)

    def normalise(b, carry):
        pltpu.make_async_copy(emb.at[b], raw.at[b], in_sem.at[b]).wait()
        nb[b] = row_scaled(raw[b].astype(jnp.float32)).astype(jnp.bfloat16)
        pltpu.make_async_copy(nb.at[b], normed.at[b], norm_sem.at[b]).start()
        return carry

    lax.fori_loop(0, BLK_DEV, normalise, 0)
    pl.semaphore_wait(barrier, jnp.where(group == 0, SLOTS - 1, SLOTS))

    def remote(slot):
        return pltpu.make_async_remote_copy(
            src_ref=out.at[slot],
            dst_ref=fetched.at[slot],
            send_sem=send_sem.at[slot],
            recv_sem=recv_sem.at[slot],
            device_id={"rows": peer_at(me, group, slot, 1)},
            device_id_type=MESH,
        )

    def send(slot, carry):
        @pl.when(is_remote(group, slot))
        def _():
            out[slot] = nb[wanted[peer_at(me, group, slot, 1)]]
            remote(slot).start()

        return carry

    lax.fori_loop(0, SLOTS, send, 0)

    def finish(slot, carry):
        @pl.when(is_remote(group, slot))
        def _():
            remote(slot).wait()

        return carry

    lax.fori_loop(0, SLOTS, finish, 0)

    def written(b, carry):
        pltpu.make_async_copy(nb.at[b], normed.at[b], norm_sem.at[b]).wait()
        return carry

    lax.fori_loop(0, BLK_DEV, written, 0)


def cubed(cosines):
    weight = jnp.maximum(cosines * (1.0 / FEATURES), 0.0)
    return (weight * weight * weight).astype(jnp.bfloat16)


def nt_dot(left, right):
    return lax.dot_general(left, right, (((1,), (1,)), ((), ())), preferred_element_type=jnp.float32)


def tn_dot(left, right):
    return lax.dot_general(left, right, (((0,), (0,)), ((), ())), preferred_element_type=jnp.float32)


def pair_kernel(links, counts, normed, fetched, totals_out, back_out, nb, got, cat, totals, back, in_sem, got_sem,
                out_sem, back_sem):
    me = lax.axis_index("rows")
    group = lax.axis_index("grp")

    def load_block(b):
        return pltpu.make_async_copy(normed.at[b], nb.at[b], in_sem.at[b])

    def load_slot(slot):
        return pltpu.make_async_copy(fetched.at[slot], got.at[slot], got_sem.at[slot])

    def store_block(b):
        return pltpu.make_async_copy(totals.at[b], totals_out.at[b], out_sem.at[b])

    def store_slot(slot):
        return pltpu.make_async_copy(back.at[slot], back_out.at[slot], back_sem.at[slot])

    def start_block(b, carry):
        load_block(lax.rem(b + group * (BLK_DEV // GROUPS), BLK_DEV)).start()
        return carry

    lax.fori_loop(0, BLK_DEV, start_block, 0)

    def start_slot(slot, carry):
        load_slot(slot).start()
        return carry

    lax.fori_loop(0, SLOTS, start_slot, 0)

    def diagonal(i, carry):
        b = group * (BLK_DEV // GROUPS) + i
        load_block(b).wait()
        block = nb[b]
        totals[b] = jnp.dot(cubed(nt_dot(block, block)), block, preferred_element_type=jnp.float32)
        return carry

    lax.fori_loop(0, BLK_DEV // GROUPS, diagonal, 0)

    def clear(i, carry):
        b = lax.rem(group * (BLK_DEV // GROUPS) + i, BLK_DEV)
        load_block(b).wait()
        totals[b] = jnp.zeros((BLOCK, FEATURES), jnp.float32)
        return carry

    lax.fori_loop(BLK_DEV // GROUPS, BLK_DEV, clear, 0)

    def visit(slot, carry):
        peer = peer_at(me, group, slot, -1)
        count = jnp.where(is_remote(group, slot), counts[peer], 0)
        load_slot(slot).wait()

        @pl.when(count == 0)
        def _():
            back[slot] = jnp.zeros((BLOCK, FEATURES), jnp.bfloat16)

        def linked(n):
            for j in range(n):
                cat[pl.ds(j * BLOCK, BLOCK)] = nb[links[peer * LINKS + j]]
            own = cat[pl.ds(0, n * BLOCK)]
            remote = got[slot]
            weight = cubed(nt_dot(own, remote))
            back[slot] = tn_dot(weight, own).astype(jnp.bfloat16)
            for j in range(n):
                picked = links[peer * LINKS + j]
                totals[picked] += jnp.dot(
                    weight[j * BLOCK:(j + 1) * BLOCK], remote, preferred_element_type=jnp.float32
                )

        for n in range(1, LINKS + 1):
            pl.when(count == n)(functools.partial(linked, n))
        store_slot(slot).start()
        return carry

    lax.fori_loop(0, SLOTS, visit, 0)

    def start_store(b, carry):
        store_block(b).start()
        return carry

    lax.fori_loop(0, BLK_DEV, start_store, 0)

    def end_store(b, carry):
        store_block(b).wait()
        return carry

    lax.fori_loop(0, BLK_DEV, end_store, 0)

    def end_slot(slot, carry):
        store_slot(slot).wait()
        return carry

    lax.fori_loop(0, SLOTS, end_slot, 0)


def combine_kernel(wanted, part, back, refined, spread, returned, part_buf, total, own, step_in, step_out, owner_in,
                   final, part_sem, back_send, back_recv, step_send, step_recv, direct_send, direct_recv, sum_send,
                   sum_recv, gather_send, gather_recv, pass_send, pass_recv, local_sem):
    me = lax.axis_index("rows")
    group = lax.axis_index("grp")
    right, left, across = (group + 1) % GROUPS, (group + 3) % GROUPS, (group + 2) % GROUPS
    per = BLK_DEV // GROUPS
    half = per // 2
    ends = (right, left)
    sides = (left, right)

    barrier = pltpu.get_barrier_semaphore()

    def greet(slot, carry):
        @pl.when(is_remote(group, slot))
        def _():
            pl.semaphore_signal(
                barrier, inc=1, device_id={"rows": peer_at(me, group, slot, 1)}, device_id_type=MESH
            )

        return carry

    lax.fori_loop(0, SLOTS, greet, 0)
    for end in ends:
        pl.semaphore_signal(barrier, inc=1, device_id={"grp": end}, device_id_type=MESH)

    def rows_of(t):
        return pl.ds(pl.multiple_of(t * CHUNK_ROWS, CHUNK_ROWS), CHUNK_ROWS)

    def part_copy(t):
        return pltpu.make_async_copy(part.at[:, rows_of(t)], part_buf.at[t % 2], part_sem.at[t % 2])

    part_copy(0).start()

    row_id = lax.broadcasted_iota(jnp.int32, (BLK_DEV * PIECE, SLOTS * PIECE), 0)
    col_id = lax.broadcasted_iota(jnp.int32, (BLK_DEV * PIECE, SLOTS * PIECE), 1)
    hot = jnp.zeros((BLK_DEV * PIECE, SLOTS * PIECE), jnp.float32)
    for slot in range(SLOTS):
        block_id = wanted[peer_at(me, group, slot, 1)]
        hit = jnp.where(row_id == block_id * PIECE + (col_id - slot * PIECE), 1.0, 0.0)
        inside = jnp.where(col_id >= slot * PIECE, 1.0, 0.0) * jnp.where(col_id < (slot + 1) * PIECE, 1.0, 0.0)
        hot = hot + hit * inside
    spread[...] = hot.astype(jnp.bfloat16)

    @pl.when(group == 0)
    def _():
        for t in range(CHUNKS):
            returned[t, 0] = jnp.zeros((CHUNK_ROWS, FEATURES), jnp.bfloat16)

    pl.semaphore_wait(barrier, jnp.where(group == 0, SLOTS - 1, SLOTS) + 2)

    def back_copy(t, slot):
        return pltpu.make_async_remote_copy(
            src_ref=back.at[slot, rows_of(t)],
            dst_ref=returned.at[t, slot],
            send_sem=back_send.at[t, slot],
            recv_sem=back_recv.at[t, slot],
            device_id={"rows": peer_at(me, group, slot, -1)},
            device_id_type=MESH,
        )

    def each_back(action):
        def one(i, carry):
            t, slot = i // SLOTS, i % SLOTS

            @pl.when(is_remote(group, slot))
            def _():
                action(back_copy(t, slot))

            return carry

        return one

    lax.fori_loop(0, CHUNKS * SLOTS, each_back(lambda copy: copy.start()), 0)

    def along(src, dst, send, recv, t, way):
        return pltpu.make_async_remote_copy(
            src_ref=src, dst_ref=dst, send_sem=send.at[t, way], recv_sem=recv.at[t, way],
            device_id={"grp": ends[way]}, device_id_type=MESH,
        )

    def step_copy(t, way):
        return along(total.at[t, pl.ds(across * per + way * half, half)], step_in.at[t, way], step_send, step_recv,
                     t, way)

    def direct_copy(t, way):
        spot = (1 - way) * half
        return along(total.at[t, pl.ds(ends[way] * per + spot, half)], owner_in.at[t, way, pl.ds(spot, half)],
                     direct_send, direct_recv, t, way)

    def sum_copy(t, way):
        return along(step_out.at[t, way], owner_in.at[t, way, pl.ds(way * half, half)], sum_send, sum_recv, t, way)

    def gather_copy(t, way):
        return along(final.at[t], refined.at[pl.ds(group * per, per), rows_of(t)], gather_send, gather_recv, t, way)

    def pass_copy(t, way):
        spot = refined.at[pl.ds(sides[way] * per + way * half, half), rows_of(t)]
        return along(spot, spot, pass_send, pass_recv, t, way)

    def local_copy(t):
        return pltpu.make_async_copy(final.at[t], refined.at[pl.ds(group * per, per), rows_of(t)], local_sem.at[t])

    def tick(t, carry):
        @pl.when(t < CHUNKS)
        def _():
            now = t

            @pl.when(now + 1 < CHUNKS)
            def _():
                part_copy(now + 1).start()

            def arrived(slot, carry):
                @pl.when(is_remote(group, slot))
                def _():
                    back_copy(now, slot).wait_recv()

                return carry

            lax.fori_loop(0, SLOTS, arrived, 0)
            part_copy(now).wait()

            def piece(g, carry):
                rows = pl.ds(pl.multiple_of(g * PIECE, PIECE), PIECE)
                came = returned[now, :, rows, :].reshape(SLOTS * PIECE, FEATURES)
                sums = jnp.dot(spread[...], came, preferred_element_type=jnp.float32)
                sums = sums.reshape(BLK_DEV, PIECE, FEATURES) + part_buf[now % 2, :, rows, :]
                total[now, :, rows, :] = sums.astype(jnp.bfloat16)
                mine = jnp.dot(
                    spread[pl.ds(pl.multiple_of(group * per * PIECE, per * PIECE), per * PIECE), :], came,
                    preferred_element_type=jnp.float32,
                )
                own[now, :, rows, :] = (
                    mine.reshape(per, PIECE, FEATURES) + part_buf[now % 2, pl.ds(group * per, per), rows, :]
                )
                return carry

            lax.fori_loop(0, CHUNK_ROWS // PIECE, piece, 0)
            for way in range(2):
                step_copy(now, way).start()
            for way in range(2):
                direct_copy(now, way).start()

        @pl.when(jnp.logical_and(t >= 1, t < CHUNKS + 1))
        def _():
            now = t - 1
            for way in range(2):
                step_copy(now, way).wait_recv()
                mine = total[now, pl.ds(ends[way] * per + way * half, half)]
                step_out[now, way] = (
                    step_in[now, way].astype(jnp.float32) + mine.astype(jnp.float32)
                ).astype(jnp.bfloat16)
                sum_copy(now, way).start()

        @pl.when(jnp.logical_and(t >= 2, t < CHUNKS + 2))
        def _():
            now = t - 2
            for way in range(2):
                direct_copy(now, way).wait_recv()
                sum_copy(now, way).wait_recv()
            for k in range(per):
                summed = (
                    own[now, k] + owner_in[now, 0, k].astype(jnp.float32) + owner_in[now, 1, k].astype(jnp.float32)
                )
                final[now, k] = row_scaled(summed).astype(jnp.bfloat16)
            for way in range(2):
                gather_copy(now, way).start()
            local_copy(now).start()

        @pl.when(t >= 3)
        def _():
            now = t - 3
            for way in range(2):
                gather_copy(now, way).wait_recv()
                pass_copy(now, way).start()

        return carry

    lax.fori_loop(0, CHUNKS + 3, tick, 0)

    def finish(t, carry):
        for way in range(2):
            pass_copy(t, way).wait_recv()
            step_copy(t, way).wait_send()
            direct_copy(t, way).wait_send()
            sum_copy(t, way).wait_send()
            gather_copy(t, way).wait_send()
            pass_copy(t, way).wait_send()
        local_copy(t).wait()
        return carry

    lax.fori_loop(0, CHUNKS, finish, 0)
    lax.fori_loop(0, CHUNKS * SLOTS, each_back(lambda copy: copy.wait_send()), 0)


def on_device(embeddings, partner, links, counts):
    blocks = (BLK_DEV, BLOCK, FEATURES)
    slots = (SLOTS, BLOCK, FEATURES)
    wanted = partner.reshape(-1)
    my_links = links.reshape(-1)
    my_counts = counts.reshape(-1)
    smem = pl.BlockSpec(memory_space=pltpu.SMEM)
    anywhere = pl.BlockSpec(memory_space=pl.ANY)
    dma = pltpu.SemaphoreType.DMA
    normed, fetched = pl.pallas_call(
        fetch_kernel,
        out_shape=(jax.ShapeDtypeStruct(blocks, jnp.bfloat16), jax.ShapeDtypeStruct(slots, jnp.bfloat16)),
        in_specs=[smem, anywhere],
        out_specs=(anywhere, anywhere),
        scratch_shapes=[
            pltpu.VMEM(blocks, jnp.bfloat16),
            pltpu.VMEM(blocks, jnp.bfloat16),
            pltpu.VMEM(slots, jnp.bfloat16),
            dma((BLK_DEV,)),
            dma((BLK_DEV,)),
            dma((SLOTS,)),
            dma((SLOTS,)),
        ],
        compiler_params=pltpu.CompilerParams(
            collective_id=0, has_side_effects=True, vmem_limit_bytes=40 * 2**20
        ),
        name="fetch",
    )(wanted, embeddings.reshape(blocks))
    part, back = pl.pallas_call(
        pair_kernel,
        out_shape=(jax.ShapeDtypeStruct(blocks, jnp.float32), jax.ShapeDtypeStruct(slots, jnp.bfloat16)),
        in_specs=[smem, smem, anywhere, anywhere],
        out_specs=(anywhere, anywhere),
        scratch_shapes=[
            pltpu.VMEM(blocks, jnp.bfloat16),
            pltpu.VMEM(slots, jnp.bfloat16),
            pltpu.VMEM((LINKS * BLOCK, FEATURES), jnp.bfloat16),
            pltpu.VMEM(blocks, jnp.float32),
            pltpu.VMEM(slots, jnp.bfloat16),
            dma((BLK_DEV,)),
            dma((SLOTS,)),
            dma((BLK_DEV,)),
            dma((SLOTS,)),
        ],
        compiler_params=pltpu.CompilerParams(vmem_limit_bytes=50 * 2**20),
        name="pairs",
    )(my_links, my_counts, normed, fetched)
    per = BLK_DEV // GROUPS
    refined = pl.pallas_call(
        combine_kernel,
        out_shape=jax.ShapeDtypeStruct(blocks, jnp.bfloat16),
        in_specs=[smem, anywhere, anywhere],
        out_specs=anywhere,
        scratch_shapes=[
            pltpu.VMEM((BLK_DEV * PIECE, SLOTS * PIECE), jnp.bfloat16),
            pltpu.VMEM((CHUNKS, SLOTS, CHUNK_ROWS, FEATURES), jnp.bfloat16),
            pltpu.VMEM((2, BLK_DEV, CHUNK_ROWS, FEATURES), jnp.float32),
            pltpu.VMEM((CHUNKS, BLK_DEV, CHUNK_ROWS, FEATURES), jnp.bfloat16),
            pltpu.VMEM((CHUNKS, per, CHUNK_ROWS, FEATURES), jnp.float32),
            pltpu.VMEM((CHUNKS, 2, per // 2, CHUNK_ROWS, FEATURES), jnp.bfloat16),
            pltpu.VMEM((CHUNKS, 2, per // 2, CHUNK_ROWS, FEATURES), jnp.bfloat16),
            pltpu.VMEM((CHUNKS, 2, per, CHUNK_ROWS, FEATURES), jnp.bfloat16),
            pltpu.VMEM((CHUNKS, per, CHUNK_ROWS, FEATURES), jnp.bfloat16),
            dma((2,)),
            dma((CHUNKS, SLOTS)),
            dma((CHUNKS, SLOTS)),
        ] + [dma((CHUNKS, 2))] * 10 + [dma((CHUNKS,))],
        compiler_params=pltpu.CompilerParams(
            collective_id=1, has_side_effects=True, vmem_limit_bytes=50 * 2**20
        ),
        name="combine",
    )(wanted, part, back)
    return refined.reshape(BLK_DEV * BLOCK, FEATURES)


def solution(mesh):
    placed = (P("rows", None), P(None, "rows"), P("rows", None, None), P("rows", None))
    return jax.shard_map(
        on_device, mesh=mesh, in_specs=placed, out_specs=P("rows", None), check_vma=False
    )
```

```python
import jax
import jax.numpy as jnp
from jax import lax
from jax.experimental import pallas as pl
from jax.experimental.pallas import tpu as pltpu
from jax.sharding import PartitionSpec as P

BLOCK = 256
FEATURES = 768
BLK_DEV = 16
LINKS = 4
GROUPS = 4
SLOTS = 8
SELF_SLOT = 6
TERMS = SLOTS * LINKS + SLOTS
CHUNKS = 4
CHUNK_ROWS = BLOCK // CHUNKS
PIECE = 16
MESH = pl.DeviceIdType.MESH


def slot_step(group, slot):
    turn = slot // 2
    ties_first = jnp.where(turn == 0, 2, jnp.where(turn == 1, 1, jnp.where(turn == 2, 3, 0)))
    step_x = jnp.where(group <= 1, ties_first, jnp.where(group == 2, turn, (turn + 2) % 4))
    return step_x, (step_x + group) % 4, slot % 2


def peer_at(me, group, slot, sign):
    step_x, step_y, flip = slot_step(group, slot)
    x, y, core = me // 8, (me // 2) % 4, me % 2
    return ((x + sign * step_x + 4) % 4) * 8 + ((y + sign * step_y + 4) % 4) * 2 + (core + flip) % 2


def is_remote(group, slot):
    return jnp.logical_or(group != 0, slot != SELF_SLOT)


def row_scaled(values):
    return values * lax.rsqrt(jnp.mean(values * values, axis=-1, keepdims=True) + 1e-06)


def cubed_float(cosines):
    weight = jnp.maximum(cosines * (1.0 / FEATURES), 0.0)
    return weight * weight * weight


def cubed(cosines):
    return cubed_float(cosines).astype(jnp.bfloat16)


def nt_dot(left, right):
    return lax.dot_general(left, right, (((1,), (1,)), ((), ())), preferred_element_type=jnp.float32)


def tn_dot(left, right):
    return lax.dot_general(left, right, (((0,), (0,)), ((), ())), preferred_element_type=jnp.float32)


def whole_kernel(wanted, links, counts, emb, refined, nb, out, fetched, cat, forward, back, spread, returned, terms, total,
                 own, step_in, step_out, owner_in, final, in_sem, fetch_send, fetch_recv, back_send, back_recv,
                 step_send, step_recv, direct_send, direct_recv, sum_send, sum_recv, gather_send, gather_recv,
                 pass_send, pass_recv, local_sem):
    me = lax.axis_index("rows")
    group = lax.axis_index("grp")
    right, left, across = (group + 1) % GROUPS, (group + 3) % GROUPS, (group + 2) % GROUPS
    per = BLK_DEV // GROUPS
    half = per // 2
    ends = (right, left)
    sides = (left, right)
    partners = jnp.where(group == 0, SLOTS - 1, SLOTS)

    def each(count, action):
        def one(i, carry):
            action(i)
            return carry

        lax.fori_loop(0, count, one, 0)

    def each_remote(action):
        def one(slot):
            @pl.when(is_remote(group, slot))
            def _():
                action(slot)

        each(SLOTS, one)

    def emb_copy(b):
        return pltpu.make_async_copy(emb.at[b], nb.at[b], in_sem.at[b])

    each(BLK_DEV, lambda b: emb_copy(b).start())
    barrier = pltpu.get_barrier_semaphore()

    def greet(slot):
        for sign in (1, -1):
            pl.semaphore_signal(
                barrier, inc=1, device_id={"rows": peer_at(me, group, slot, sign)}, device_id_type=MESH
            )

    each_remote(greet)
    for end in ends:
        pl.semaphore_signal(barrier, inc=1, device_id={"grp": end}, device_id_type=MESH)

    def normalise(b):
        emb_copy(b).wait()
        nb[b] = row_scaled(nb[b].astype(jnp.float32)).astype(jnp.bfloat16)

    each(BLK_DEV, normalise)

    @pl.when(group == 0)
    def _():
        fetched[SELF_SLOT] = jnp.zeros((BLOCK, FEATURES), jnp.bfloat16)
        for t in range(CHUNKS):
            returned[t, SELF_SLOT] = jnp.zeros((CHUNK_ROWS, FEATURES), jnp.bfloat16)

    pl.semaphore_wait(barrier, 2 * partners + 2)

    def fetch_copy(slot):
        return pltpu.make_async_remote_copy(
            src_ref=out.at[slot],
            dst_ref=fetched.at[slot],
            send_sem=fetch_send.at[slot],
            recv_sem=fetch_recv.at[slot],
            device_id={"rows": peer_at(me, group, slot, 1)},
            device_id_type=MESH,
        )

    def send(slot):
        out[slot] = nb[wanted[peer_at(me, group, slot, 1)]]
        fetch_copy(slot).start()

    each_remote(send)

    def diagonal(k):
        block = nb[group * per + k]
        own[k] = jnp.dot(cubed(nt_dot(block, block)), block, preferred_element_type=jnp.float32)

    each(per, diagonal)

    col = lax.broadcasted_iota(jnp.int32, (8, TERMS * PIECE), 1)
    takes = jnp.zeros((8, TERMS * PIECE), jnp.int32)
    for slot in range(SLOTS):
        lister = peer_at(me, group, slot, 1)
        listed = peer_at(me, group, slot, -1)
        for j in range(LINKS):
            takes = jnp.where(col // PIECE == slot * LINKS + j, links[listed * LINKS + j], takes)
        takes = jnp.where(col // PIECE == SLOTS * LINKS + slot, wanted[lister], takes)
    row_id = lax.broadcasted_iota(jnp.int32, (BLK_DEV * PIECE, TERMS * PIECE), 0)
    col_id = lax.broadcasted_iota(jnp.int32, (BLK_DEV * PIECE, TERMS * PIECE), 1)
    spread[...] = jnp.where(row_id == takes[0:1] * PIECE + col_id % PIECE, 1.0, 0.0).astype(jnp.bfloat16)

    def rows_of(t):
        return pl.ds(pl.multiple_of(t * CHUNK_ROWS, CHUNK_ROWS), CHUNK_ROWS)

    def back_copy(t, slot):
        return pltpu.make_async_remote_copy(
            src_ref=back.at[slot, rows_of(t)],
            dst_ref=returned.at[t, slot],
            send_sem=back_send.at[t, slot],
            recv_sem=back_recv.at[t, slot],
            device_id={"rows": peer_at(me, group, slot, -1)},
            device_id_type=MESH,
        )

    row_number = lax.broadcasted_iota(jnp.int32, (LINKS * BLOCK, BLOCK), 0)

    def visit(slot):
        peer = peer_at(me, group, slot, -1)

        @pl.when(is_remote(group, slot))
        def _():
            fetch_copy(slot).wait_recv()

        for j in range(LINKS):
            cat[j * BLOCK:(j + 1) * BLOCK] = nb[links[peer * LINKS + j]]
        remote = fetched[slot]
        weight = jnp.where(
            row_number < counts[peer] * BLOCK, cubed_float(nt_dot(cat[...], remote)), 0.0
        ).astype(jnp.bfloat16)
        back[slot] = tn_dot(weight, cat[...]).astype(jnp.bfloat16)

        @pl.when(is_remote(group, slot))
        def _():
            back_copy(0, slot).start()

        for j in range(LINKS):
            forward[slot * LINKS + j] = jnp.dot(
                weight[j * BLOCK:(j + 1) * BLOCK], remote, preferred_element_type=jnp.float32
            ).astype(jnp.bfloat16)

    each(SLOTS, visit)
    for t in range(1, CHUNKS):
        each_remote(lambda slot: back_copy(t, slot).start())

    def along(src, dst, send, recv, t, way):
        return pltpu.make_async_remote_copy(
            src_ref=src, dst_ref=dst, send_sem=send.at[t, way], recv_sem=recv.at[t, way],
            device_id={"grp": ends[way]}, device_id_type=MESH,
        )

    def step_copy(t, way):
        return along(total.at[t, pl.ds(across * per + way * half, half)], step_in.at[t, way], step_send, step_recv,
                     t, way)

    def direct_copy(t, way):
        spot = (1 - way) * half
        return along(total.at[t, pl.ds(ends[way] * per + spot, half)], owner_in.at[t, way, pl.ds(spot, half)],
                     direct_send, direct_recv, t, way)

    def sum_copy(t, way):
        return along(step_out.at[t, way], owner_in.at[t, way, pl.ds(way * half, half)], sum_send, sum_recv, t, way)

    def gather_copy(t, way):
        return along(final.at[t], refined.at[pl.ds(group * per, per), rows_of(t)], gather_send, gather_recv, t, way)

    def pass_copy(t, way):
        spot = refined.at[pl.ds(sides[way] * per + way * half, half), rows_of(t)]
        return along(spot, spot, pass_send, pass_recv, t, way)

    def local_copy(t):
        return pltpu.make_async_copy(final.at[t], refined.at[pl.ds(group * per, per), rows_of(t)], local_sem.at[t])

    def tick(t, carry):
        @pl.when(t < CHUNKS)
        def _():
            now = t

            each_remote(lambda slot: back_copy(now, slot).wait_recv())

            def piece(g):
                rows = pl.ds(pl.multiple_of(g * PIECE, PIECE), PIECE)
                whole_rows = pl.ds(pl.multiple_of(now * CHUNK_ROWS + g * PIECE, PIECE), PIECE)
                terms[0:SLOTS * LINKS * PIECE] = forward[:, whole_rows, :].reshape(SLOTS * LINKS * PIECE, FEATURES)
                terms[SLOTS * LINKS * PIECE:] = returned[now, :, rows, :].reshape(SLOTS * PIECE, FEATURES)
                sums = jnp.dot(spread[...], terms[...], preferred_element_type=jnp.float32)
                total[now, :, rows, :] = sums.reshape(BLK_DEV, PIECE, FEATURES).astype(jnp.bfloat16)
                mine = jnp.dot(
                    spread[pl.ds(pl.multiple_of(group * per * PIECE, per * PIECE), per * PIECE), :], terms[...],
                    preferred_element_type=jnp.float32,
                )
                own[:, whole_rows, :] += mine.reshape(per, PIECE, FEATURES)

            each(CHUNK_ROWS // PIECE, piece)
            for way in range(2):
                step_copy(now, way).start()
            for way in range(2):
                direct_copy(now, way).start()

        @pl.when(jnp.logical_and(t >= 1, t < CHUNKS + 1))
        def _():
            now = t - 1
            for way in range(2):
                step_copy(now, way).wait_recv()
                mine = total[now, pl.ds(ends[way] * per + way * half, half)]
                step_out[now, way] = (
                    step_in[now, way].astype(jnp.float32) + mine.astype(jnp.float32)
                ).astype(jnp.bfloat16)
                sum_copy(now, way).start()

        @pl.when(jnp.logical_and(t >= 2, t < CHUNKS + 2))
        def _():
            now = t - 2
            for way in range(2):
                direct_copy(now, way).wait_recv()
                sum_copy(now, way).wait_recv()
            for k in range(per):
                summed = (
                    own[k, rows_of(now)] + owner_in[now, 0, k].astype(jnp.float32) + owner_in[now, 1, k].astype(jnp.float32)
                )
                final[now, k] = row_scaled(summed).astype(jnp.bfloat16)
            for way in range(2):
                gather_copy(now, way).start()
            local_copy(now).start()

        @pl.when(t >= 3)
        def _():
            now = t - 3
            for way in range(2):
                gather_copy(now, way).wait_recv()
                pass_copy(now, way).start()

        return carry

    lax.fori_loop(0, CHUNKS + 3, tick, 0)

    def finish(t, carry):
        for way in range(2):
            pass_copy(t, way).wait_recv()
            step_copy(t, way).wait_send()
            direct_copy(t, way).wait_send()
            sum_copy(t, way).wait_send()
            gather_copy(t, way).wait_send()
            pass_copy(t, way).wait_send()
        local_copy(t).wait()
        return carry

    lax.fori_loop(0, CHUNKS, finish, 0)
    each_remote(lambda slot: fetch_copy(slot).wait_send())
    for t in range(CHUNKS):
        each_remote(lambda slot: back_copy(t, slot).wait_send())


def on_device(embeddings, partner, links, counts):
    blocks = (BLK_DEV, BLOCK, FEATURES)
    slots = (SLOTS, BLOCK, FEATURES)
    per = BLK_DEV // GROUPS
    smem = pl.BlockSpec(memory_space=pltpu.SMEM)
    dma = pltpu.SemaphoreType.DMA

    def vmem(*shape):
        return pltpu.VMEM(shape + (FEATURES,), jnp.bfloat16)

    refined = pl.pallas_call(
        whole_kernel,
        out_shape=jax.ShapeDtypeStruct(blocks, jnp.bfloat16),
        in_specs=[smem, smem, smem, pl.BlockSpec(memory_space=pl.ANY)],
        out_specs=pl.BlockSpec(memory_space=pl.ANY),
        scratch_shapes=[
            vmem(BLK_DEV, BLOCK),
            vmem(SLOTS, BLOCK),
            vmem(SLOTS, BLOCK),
            vmem(LINKS * BLOCK),
            vmem(SLOTS * LINKS, BLOCK),
            vmem(SLOTS, BLOCK),
            pltpu.VMEM((BLK_DEV * PIECE, TERMS * PIECE), jnp.bfloat16),
            vmem(CHUNKS, SLOTS, CHUNK_ROWS),
            vmem(TERMS * PIECE),
            vmem(CHUNKS, BLK_DEV, CHUNK_ROWS),
            pltpu.VMEM((per, BLOCK, FEATURES), jnp.float32),
            vmem(CHUNKS, 2, per // 2, CHUNK_ROWS),
            vmem(CHUNKS, 2, per // 2, CHUNK_ROWS),
            vmem(CHUNKS, 2, per, CHUNK_ROWS),
            vmem(CHUNKS, per, CHUNK_ROWS),
            dma((BLK_DEV,)),
            dma((SLOTS,)),
            dma((SLOTS,)),
            dma((CHUNKS, SLOTS)),
            dma((CHUNKS, SLOTS)),
        ] + [dma((CHUNKS, 2))] * 10 + [dma((CHUNKS,))],
        compiler_params=pltpu.CompilerParams(
            collective_id=0, has_side_effects=True, vmem_limit_bytes=62 * 2**20
        ),
        name="whole",
    )(partner.reshape(-1), links.reshape(-1), counts.reshape(-1), embeddings.reshape(blocks))
    return refined.reshape(BLK_DEV * BLOCK, FEATURES)


def solution(mesh):
    placed = (P("rows", None), P(None, "rows"), P("rows", None, None), P("rows", None))
    return jax.shard_map(
        on_device, mesh=mesh, in_specs=placed, out_specs=P("rows", None), check_vma=False
    )
```

```python
import jax
import jax.numpy as jnp
from jax import lax
from jax.experimental import pallas as pl
from jax.experimental.pallas import tpu as pltpu
from jax.sharding import PartitionSpec as P

BLOCK = 256
FEATURES = 768
BLK_DEV = 16
HALF = BLK_DEV // 2
LINKS = 4
PLANES = 4
SLOTS = 16
ROUND = 4
CHUNKS = 4
CHUNK_ROWS = BLOCK // CHUNKS
PIECE = 16
NEAR = 6
MESH = pl.DeviceIdType.MESH


def slot_at(turn):
    diagonal, step = turn // 4, turn % 4
    ties_first = jnp.where(step == 0, 2, jnp.where(step == 1, 1, jnp.where(step == 2, 3, 0)))
    step_x = jnp.where(diagonal <= 1, ties_first, jnp.where(diagonal == 2, step, (step + 2) % 4))
    return step_x * 4 + (step_x + diagonal) % 4


def live_core(parity, plane):
    upper = (plane + 4 - parity) % 2
    return ((plane + 8 - upper - parity) % 4) // 2


def idle_side(slot, upper):
    step_x, step_y = slot // 4, slot % 4
    return jnp.where((step_x + step_y) % 2 == 0, (step_x + upper + 1) % 2, 0)


def crossed(slot, idle):
    step_x, step_y = slot // 4, slot % 4
    return jnp.where(idle == 1, (step_x + 1 - 2 * (step_x % 2)) * 4 + step_y + 1 - 2 * (step_y % 2), slot)


def row_scaled(values):
    return values * lax.rsqrt(jnp.mean(values * values, axis=-1, keepdims=True) + 1e-06)


def cubed(cosines):
    weight = jnp.maximum(cosines * (1.0 / FEATURES), 0.0)
    return weight * weight * weight


def nt_dot(left, right):
    return lax.dot_general(left, right, (((1,), (1,)), ((), ())), preferred_element_type=jnp.float32)


def tn_dot(left, right):
    return lax.dot_general(left, right, (((0,), (0,)), ((), ())), preferred_element_type=jnp.float32)


def whole_kernel(wanted, links, counts, emb, refined, nb, out, fetched, cat, forward, totals, back, spread, returned,
                 half_in, in_sem, fetch_send, fetch_recv, back_send, back_recv, half_send, half_recv, pair_send,
                 pair_recv, next_send, next_recv, near_send, near_recv, far_send, far_recv, local_sem):
    me = lax.axis_index("rows")
    plane = lax.axis_index("grp")
    x, y, core = me // 8, (me // 2) % 4, me % 2
    parity = (x + y) % 2
    role = (plane + 4 - (2 * core + parity)) % 4
    live = role < 2
    upper = (plane + 4 - parity) % 2
    mine = jnp.where(jnp.logical_or(role == 1, role == 2), 1, 0)
    inner = (plane + 5 - 2 * mine) % PLANES
    outer = (plane + 3 + 2 * mine) % PLANES

    def each(count, action):
        def one(i, carry):
            action(i)
            return carry

        lax.fori_loop(0, count, one, 0)

    def each_slot(action):
        def one(turn):
            slot = slot_at(turn)

            @pl.when(not_self(slot))
            def _():
                action(slot)

        each(SLOTS, one)

    def not_self(slot):
        return jnp.logical_or(slot != 0, upper == 0)

    def chip(slot, sign):
        step_x, step_y = slot // 4, slot % 4
        there = ((x + sign * step_x + 4) % 4) * 8 + ((y + sign * step_y + 4) % 4) * 2
        return there, (parity + step_x + step_y) % 2

    def owner_of(slot):
        there, kind = chip(slot, -1)
        return there + (live_core(kind, plane) + idle_side(slot, upper)) % 2

    def owner_plane(slot):
        return (plane + 4 + idle_side(slot, upper) * (2 * upper - 1)) % PLANES

    def taker_of(slot):
        there, kind = chip(slot, 1)
        return there + live_core(kind, plane)

    def lister_of(slot):
        there, kind = chip(crossed(slot, idle_side(slot, upper)), 1)
        return there + live_core(kind, owner_plane(slot))

    def emb_copy(b):
        return pltpu.make_async_copy(emb.at[b], nb.at[b], in_sem.at[b])

    each(BLK_DEV, lambda b: emb_copy(b).start())
    barrier = pltpu.get_barrier_semaphore()

    @pl.when(live)
    def _():
        def greet(slot):
            pl.semaphore_signal(
                barrier, inc=1, device_id={"rows": owner_of(slot), "grp": plane}, device_id_type=MESH
            )
            pl.semaphore_signal(
                barrier, inc=1, device_id={"rows": lister_of(slot), "grp": owner_plane(slot)}, device_id_type=MESH
            )

        each_slot(greet)

    for side in (inner, outer):
        pl.semaphore_signal(barrier, inc=1, device_id={"rows": me, "grp": side}, device_id_type=MESH)

    each(BLK_DEV, lambda b: emb_copy(b).wait())
    pl.semaphore_wait(barrier, jnp.where(live, 30 - 2 * upper, 6))

    def fetch_copy(slot):
        return pltpu.make_async_remote_copy(
            src_ref=out.at[slot],
            dst_ref=fetched.at[slot],
            send_sem=fetch_send.at[slot],
            recv_sem=fetch_recv.at[slot],
            device_id={"rows": taker_of(slot), "grp": plane},
            device_id_type=MESH,
        )

    def each_sent(action):
        def one(slot):
            @pl.when(idle_side(slot, upper) == jnp.where(live, 0, 1))
            def _():
                action(slot)

        each_slot(one)

    def send(slot):
        out[slot] = row_scaled(nb[wanted[taker_of(slot)]].astype(jnp.float32)).astype(jnp.bfloat16)
        fetch_copy(slot).start()

    each_sent(send)

    def rows_of(t):
        return pl.ds(pl.multiple_of(t * CHUNK_ROWS, CHUNK_ROWS), CHUNK_ROWS)

    def back_copy(t, slot):
        idle = idle_side(slot, upper)
        return pltpu.make_async_remote_copy(
            src_ref=back.at[slot, rows_of(t)],
            dst_ref=returned.at[t, crossed(slot, idle)],
            send_sem=back_send.at[t, slot],
            recv_sem=back_recv.at[t, crossed(slot, idle)],
            device_id={"rows": owner_of(slot), "grp": owner_plane(slot)},
            device_id_type=MESH,
        )

    def back_arrival(t, slot):
        return pltpu.make_async_remote_copy(
            src_ref=back.at[slot, rows_of(t)],
            dst_ref=returned.at[t, slot],
            send_sem=back_send.at[t, slot],
            recv_sem=back_recv.at[t, slot],
            device_id={"rows": lister_of(slot), "grp": owner_plane(slot)},
            device_id_type=MESH,
        )

    def one_hot(block_of):
        col = lax.broadcasted_iota(jnp.int32, (8, SLOTS * PIECE), 1)
        takes = jnp.zeros((8, SLOTS * PIECE), jnp.int32)
        for term in range(SLOTS):
            takes = jnp.where(col // PIECE == term, (block_of(term) + HALF * mine) % BLK_DEV, takes)
        row_id = lax.broadcasted_iota(jnp.int32, (BLK_DEV * PIECE, SLOTS * PIECE), 0)
        col_id = lax.broadcasted_iota(jnp.int32, (BLK_DEV * PIECE, SLOTS * PIECE), 1)
        return jnp.where(row_id == takes[0:1] * PIECE + col_id % PIECE, 1.0, 0.0).astype(jnp.bfloat16)

    @pl.when(live)
    def _():
        def normalise(b):
            nb[b] = row_scaled(nb[b].astype(jnp.float32)).astype(jnp.bfloat16)

        each(BLK_DEV, normalise)

        @pl.when(upper == 1)
        def _():
            fetched[0] = jnp.zeros((BLOCK, FEATURES), jnp.bfloat16)
            for t in range(CHUNKS):
                returned[t, 0] = jnp.zeros((CHUNK_ROWS, FEATURES), jnp.bfloat16)

        def diagonal(k):
            block = nb[mine * HALF + k]
            weight = cubed(nt_dot(block, block)).astype(jnp.bfloat16)
            totals[k] = jnp.dot(weight, block, preferred_element_type=jnp.float32)
            totals[HALF + k] = jnp.zeros((BLOCK, FEATURES), jnp.float32)

        each(HALF, diagonal)
        spread[SLOTS // ROUND] = one_hot(lambda term: wanted[lister_of(term)])
        for turn in range(SLOTS // ROUND):
            spread[turn] = one_hot(
                lambda term: links[owner_of(slot_at(turn * ROUND + term // LINKS)) * LINKS + term % LINKS]
            )
        link_col = lax.broadcasted_iota(jnp.int32, (BLOCK, LINKS * BLOCK), 1)

        def visit(turn, step):
            slot = slot_at(turn * ROUND + step)
            peer = owner_of(slot)

            @pl.when(not_self(slot))
            def _():
                fetch_copy(slot).wait_recv()

            for j in range(LINKS):
                cat[j * BLOCK:(j + 1) * BLOCK] = nb[links[peer * LINKS + j]]
            remote = fetched[slot]
            weight = jnp.where(
                link_col < counts[peer] * BLOCK, cubed(nt_dot(remote, cat[...])), 0.0
            ).astype(jnp.bfloat16)
            back[slot] = jnp.dot(weight, cat[...], preferred_element_type=jnp.float32).astype(jnp.bfloat16)

            @pl.when(not_self(slot))
            def _():
                back_copy(0, slot).start()

            forward[pl.ds(step * LINKS, LINKS)] = (
                tn_dot(weight, remote).astype(jnp.bfloat16).reshape(LINKS, BLOCK, FEATURES)
            )

        def work(turn):
            each(ROUND, lambda step: visit(turn, step))

            def piece(g):
                rows = pl.ds(pl.multiple_of(g * PIECE, PIECE), PIECE)
                terms = forward[:, rows, :].reshape(ROUND * LINKS * PIECE, FEATURES)
                sums = jnp.dot(spread[turn], terms, preferred_element_type=jnp.float32)
                totals[:, rows, :] += sums.reshape(BLK_DEV, PIECE, FEATURES)

            each(BLOCK // PIECE, piece)

        each(SLOTS // ROUND, work)
        for t in range(1, CHUNKS):
            each_slot(lambda slot: back_copy(t, slot).start())

    def along(src, dst, send, recv, t, side):
        return pltpu.make_async_remote_copy(
            src_ref=src, dst_ref=dst, send_sem=send.at[t], recv_sem=recv.at[t],
            device_id={"rows": me, "grp": side}, device_id_type=MESH,
        )

    def half_copy(t):
        return along(nb.at[pl.ds(0, HALF), rows_of(t)], half_in.at[:, rows_of(t)], half_send, half_recv, t, inner)

    def result(t):
        return nb.at[pl.ds(HALF, HALF), rows_of(t)]

    def out_half(t, which):
        return refined.at[pl.ds(which * HALF, HALF), rows_of(t)]

    def pair_copy(t):
        return along(result(t), out_half(t, mine), pair_send, pair_recv, t, inner)

    def next_copy(t):
        return along(result(t), out_half(t, mine), next_send, next_recv, t, outer)

    def near_copy(t):
        spot = refined.at[pl.ds((1 - mine) * HALF, NEAR), rows_of(t)]
        return along(spot, spot, near_send, near_recv, t, outer)

    def far_copy(t):
        spot = refined.at[pl.ds(mine * HALF + NEAR, HALF - NEAR), rows_of(t)]
        return along(spot, spot, far_send, far_recv, t, outer)

    def local_copy(t):
        return pltpu.make_async_copy(result(t), out_half(t, mine), local_sem.at[t])

    @pl.when(live)
    def _():
        def tick(t):
            @pl.when(t < CHUNKS)
            def _():
                each_slot(lambda slot: back_arrival(t, slot).wait_recv())

                def piece(g):
                    rows = pl.ds(pl.multiple_of(g * PIECE, PIECE), PIECE)
                    spot = pl.ds(pl.multiple_of(t * CHUNK_ROWS + g * PIECE, PIECE), PIECE)
                    came = returned[t, :, rows, :].reshape(SLOTS * PIECE, FEATURES)
                    sums = jnp.dot(spread[SLOTS // ROUND], came, preferred_element_type=jnp.float32)
                    sums = sums.reshape(BLK_DEV, PIECE, FEATURES)
                    totals[0:HALF, spot, :] += sums[0:HALF]
                    nb[0:HALF, spot, :] = (totals[HALF:BLK_DEV, spot, :] + sums[HALF:BLK_DEV]).astype(jnp.bfloat16)

                each(CHUNK_ROWS // PIECE, piece)
                half_copy(t).start()

            @pl.when(jnp.logical_and(t >= 1, t < CHUNKS + 1))
            def _():
                now = t - 1
                half_copy(now).wait_recv()

                def finish_block(k):
                    summed = totals[k, rows_of(now), :] + half_in[k, rows_of(now), :].astype(jnp.float32)
                    nb[HALF + k, rows_of(now), :] = row_scaled(summed).astype(jnp.bfloat16)

                each(HALF, finish_block)
                pair_copy(now).start()
                next_copy(now).start()
                local_copy(now).start()

            @pl.when(t >= 2)
            def _():
                pair_copy(t - 2).wait_recv()
                near_copy(t - 2).start()

        each(CHUNKS + 2, tick)

        def finish(t):
            half_copy(t).wait_send()
            pair_copy(t).wait_send()
            next_copy(t).wait_send()
            near_copy(t).wait_send()
            local_copy(t).wait()

        each(CHUNKS, finish)
        for t in range(CHUNKS):
            each_slot(lambda slot: back_copy(t, slot).wait_send())

    @pl.when(jnp.logical_not(live))
    def _():
        def tick(t):
            next_copy(t).wait_recv()
            far_copy(t).start()

        each(CHUNKS, tick)

        def finish(t):
            near_copy(t).wait_recv()
            far_copy(t).wait()

        each(CHUNKS, finish)

    each_sent(lambda slot: fetch_copy(slot).wait_send())


def on_device(embeddings, partner, links, counts):
    blocks = (BLK_DEV, BLOCK, FEATURES)
    smem = pl.BlockSpec(memory_space=pltpu.SMEM)
    dma = pltpu.SemaphoreType.DMA

    def vmem(*shape):
        return pltpu.VMEM(shape + (FEATURES,), jnp.bfloat16)

    refined = pl.pallas_call(
        whole_kernel,
        out_shape=jax.ShapeDtypeStruct(blocks, jnp.bfloat16),
        in_specs=[smem, smem, smem, pl.BlockSpec(memory_space=pl.ANY)],
        out_specs=pl.BlockSpec(memory_space=pl.ANY),
        scratch_shapes=[
            vmem(BLK_DEV, BLOCK),
            vmem(SLOTS, BLOCK),
            vmem(SLOTS, BLOCK),
            vmem(LINKS * BLOCK),
            vmem(ROUND * LINKS, BLOCK),
            pltpu.VMEM(blocks, jnp.float32),
            vmem(SLOTS, BLOCK),
            pltpu.VMEM((SLOTS // ROUND + 1, BLK_DEV * PIECE, SLOTS * PIECE), jnp.bfloat16),
            vmem(CHUNKS, SLOTS, CHUNK_ROWS),
            vmem(HALF, BLOCK),
            dma((BLK_DEV,)),
            dma((SLOTS,)),
            dma((SLOTS,)),
            dma((CHUNKS, SLOTS)),
            dma((CHUNKS, SLOTS)),
        ] + [dma((CHUNKS,))] * 11,
        compiler_params=pltpu.CompilerParams(
            collective_id=0, has_side_effects=True, vmem_limit_bytes=62 * 2**20
        ),
        name="whole",
    )(partner.reshape(-1), links.reshape(-1), counts.reshape(-1), embeddings.reshape(blocks))
    return refined.reshape(BLK_DEV * BLOCK, FEATURES)


def solution(mesh):
    placed = (P("rows", None), P(None, "rows"), P("rows", None, None), P("rows", None))
    return jax.shard_map(
        on_device, mesh=mesh, in_specs=placed, out_specs=P("rows", None), check_vma=False
    )
```

```python
import jax
import jax.numpy as jnp
from jax import lax
from jax.experimental import pallas as pl
from jax.experimental.pallas import tpu as pltpu
from jax.sharding import PartitionSpec as P

BLOCK = 256
FEATURES = 768
BLK_DEV = 16
HALF = BLK_DEV // 2
LINKS = 4
PLANES = 4
SLOTS = 16
CHUNKS = 8
CHUNK_ROWS = BLOCK // CHUNKS
BACKS = 4
BACK_ROWS = BLOCK // BACKS
WIDER = CHUNKS // BACKS
PIECE = 16
NEAR = 6
MESH = pl.DeviceIdType.MESH


def slot_at(turn):
    diagonal, step = turn // 4, turn % 4
    ties_first = jnp.where(step == 0, 2, jnp.where(step == 1, 1, jnp.where(step == 2, 3, 0)))
    step_x = jnp.where(diagonal <= 1, ties_first, jnp.where(diagonal == 2, step, (step + 2) % 4))
    return step_x * 4 + (step_x + diagonal) % 4


def live_core(parity, plane):
    upper = (plane + 4 - parity) % 2
    return ((plane + 8 - upper - parity) % 4) // 2


def idle_side(slot, upper):
    step_x, step_y = slot // 4, slot % 4
    return jnp.where((step_x + step_y) % 2 == 0, (step_x + upper + 1) % 2, 0)


def crossed(slot, idle):
    step_x, step_y = slot // 4, slot % 4
    return jnp.where(idle == 1, (step_x + 1 - 2 * (step_x % 2)) * 4 + step_y + 1 - 2 * (step_y % 2), slot)


def row_scaled(values):
    return values * lax.rsqrt(jnp.mean(values * values, axis=-1, keepdims=True) + 1e-06)


def cubed(cosines):
    weight = jnp.maximum(cosines * (1.0 / FEATURES), 0.0)
    return weight * weight * weight


def nt_dot(left, right):
    return lax.dot_general(left, right, (((1,), (1,)), ((), ())), preferred_element_type=jnp.float32)


def tn_dot(left, right):
    return lax.dot_general(left, right, (((0,), (0,)), ((), ())), preferred_element_type=jnp.float32)


def whole_kernel(wanted, links, counts, emb, refined, nb, out, fetched, cat, kept, forward, totals, back, spread,
                 back_spread, returned,
                 half_in, in_sem, fetch_send, fetch_recv, back_send, back_recv, half_send, half_recv, pair_send,
                 pair_recv, next_send, next_recv, near_send, near_recv, far_send, far_recv, local_sem):
    me = lax.axis_index("rows")
    plane = lax.axis_index("grp")
    x, y, core = me // 8, (me // 2) % 4, me % 2
    parity = (x + y) % 2
    role = (plane + 4 - (2 * core + parity)) % 4
    live = role < 2
    upper = (plane + 4 - parity) % 2
    mine = jnp.where(jnp.logical_or(role == 1, role == 2), 1, 0)
    inner = (plane + 5 - 2 * mine) % PLANES
    outer = (plane + 3 + 2 * mine) % PLANES

    def each(count, action):
        def one(i, carry):
            action(i)
            return carry

        lax.fori_loop(0, count, one, 0)

    def each_slot(action):
        def one(turn):
            slot = slot_at(turn)

            @pl.when(not_self(slot))
            def _():
                action(slot)

        each(SLOTS, one)

    def not_self(slot):
        return jnp.logical_or(slot != 0, upper == 0)

    def chip(slot, sign):
        step_x, step_y = slot // 4, slot % 4
        there = ((x + sign * step_x + 4) % 4) * 8 + ((y + sign * step_y + 4) % 4) * 2
        return there, (parity + step_x + step_y) % 2

    def owner_of(slot):
        there, kind = chip(slot, -1)
        return there + (live_core(kind, plane) + idle_side(slot, upper)) % 2

    def owner_plane(slot):
        return (plane + 4 + idle_side(slot, upper) * (2 * upper - 1)) % PLANES

    def taker_of(slot):
        there, kind = chip(slot, 1)
        return there + live_core(kind, plane)

    def lister_of(slot):
        there, kind = chip(crossed(slot, idle_side(slot, upper)), 1)
        return there + live_core(kind, owner_plane(slot))

    def emb_copy(b):
        return pltpu.make_async_copy(emb.at[b], nb.at[b], in_sem.at[b])

    each(BLK_DEV, lambda b: emb_copy(b).start())
    barrier = pltpu.get_barrier_semaphore()

    @pl.when(live)
    def _():
        def greet(slot):
            pl.semaphore_signal(
                barrier, inc=1, device_id={"rows": owner_of(slot), "grp": plane}, device_id_type=MESH
            )
            pl.semaphore_signal(
                barrier, inc=1, device_id={"rows": lister_of(slot), "grp": owner_plane(slot)}, device_id_type=MESH
            )

        each_slot(greet)

    for side in (inner, outer):
        pl.semaphore_signal(barrier, inc=1, device_id={"rows": me, "grp": side}, device_id_type=MESH)

    each(BLK_DEV, lambda b: emb_copy(b).wait())
    pl.semaphore_wait(barrier, jnp.where(live, 30 - 2 * upper, 6))

    def fetch_copy(slot):
        return pltpu.make_async_remote_copy(
            src_ref=out.at[slot],
            dst_ref=fetched.at[slot],
            send_sem=fetch_send.at[slot],
            recv_sem=fetch_recv.at[slot],
            device_id={"rows": taker_of(slot), "grp": plane},
            device_id_type=MESH,
        )

    def each_sent(action):
        def one(slot):
            @pl.when(idle_side(slot, upper) == jnp.where(live, 0, 1))
            def _():
                action(slot)

        each_slot(one)

    def send(slot):
        out[slot] = row_scaled(nb[wanted[taker_of(slot)]].astype(jnp.float32)).astype(jnp.bfloat16)
        fetch_copy(slot).start()

    each_sent(send)

    def rows_of(t):
        return pl.ds(pl.multiple_of(t * CHUNK_ROWS, CHUNK_ROWS), CHUNK_ROWS)

    def back_rows(t):
        return pl.ds(pl.multiple_of(t * BACK_ROWS, BACK_ROWS), BACK_ROWS)

    def back_copy(t, slot):
        idle = idle_side(slot, upper)
        return pltpu.make_async_remote_copy(
            src_ref=back.at[slot, back_rows(t)],
            dst_ref=returned.at[t, crossed(slot, idle)],
            send_sem=back_send.at[t, slot],
            recv_sem=back_recv.at[t, crossed(slot, idle)],
            device_id={"rows": owner_of(slot), "grp": owner_plane(slot)},
            device_id_type=MESH,
        )

    def back_arrival(t, slot):
        return pltpu.make_async_remote_copy(
            src_ref=back.at[slot, back_rows(t)],
            dst_ref=returned.at[t, slot],
            send_sem=back_send.at[t, slot],
            recv_sem=back_recv.at[t, slot],
            device_id={"rows": lister_of(slot), "grp": owner_plane(slot)},
            device_id_type=MESH,
        )

    def one_hot(block_of, count):
        col = lax.broadcasted_iota(jnp.int32, (8, count * PIECE), 1)
        takes = jnp.zeros((8, count * PIECE), jnp.int32)
        for term in range(count):
            takes = jnp.where(col // PIECE == term, (block_of(term) + HALF * mine) % BLK_DEV, takes)
        row_id = lax.broadcasted_iota(jnp.int32, (BLK_DEV * PIECE, count * PIECE), 0)
        col_id = lax.broadcasted_iota(jnp.int32, (BLK_DEV * PIECE, count * PIECE), 1)
        return jnp.where(row_id == takes[0:1] * PIECE + col_id % PIECE, 1.0, 0.0).astype(jnp.bfloat16)

    @pl.when(live)
    def _():
        def normalise(b):
            nb[b] = row_scaled(nb[b].astype(jnp.float32)).astype(jnp.bfloat16)

        each(BLK_DEV, normalise)

        @pl.when(upper == 1)
        def _():
            fetched[0] = jnp.zeros((BLOCK, FEATURES), jnp.bfloat16)
            for t in range(BACKS):
                returned[t, 0] = jnp.zeros((BACK_ROWS, FEATURES), jnp.bfloat16)

        def diagonal(k):
            block = nb[mine * HALF + k]
            weight = cubed(nt_dot(block, block)).astype(jnp.bfloat16)
            totals[k] = jnp.dot(weight, block, preferred_element_type=jnp.float32)

        each(HALF, diagonal)
        back_spread[...] = one_hot(lambda term: wanted[lister_of(term)], SLOTS)
        spread[...] = one_hot(lambda term: links[owner_of(term // LINKS) * LINKS + term % LINKS], SLOTS * LINKS)
        link_col = lax.broadcasted_iota(jnp.int32, (BLOCK, LINKS * BLOCK), 1)

        def visit(turn):
            slot = slot_at(turn)
            peer = owner_of(slot)

            @pl.when(not_self(slot))
            def _():
                fetch_copy(slot).wait_recv()

            for j in range(LINKS):
                cat[j * BLOCK:(j + 1) * BLOCK] = nb[links[peer * LINKS + j]]
            weight = jnp.where(
                link_col < counts[peer] * BLOCK, cubed(nt_dot(fetched[slot], cat[...])), 0.0
            ).astype(jnp.bfloat16)
            back[slot] = jnp.dot(weight, cat[...], preferred_element_type=jnp.float32).astype(jnp.bfloat16)

            @pl.when(not_self(slot))
            def _():
                back_copy(0, slot).start()

            kept[slot] = weight.T.reshape(LINKS, BLOCK, BLOCK)

        each(SLOTS, visit)
        for t in range(1, BACKS):
            each_slot(lambda slot: back_copy(t, slot).start())

    def along(src, dst, send, recv, t, side):
        return pltpu.make_async_remote_copy(
            src_ref=src, dst_ref=dst, send_sem=send.at[t], recv_sem=recv.at[t],
            device_id={"rows": me, "grp": side}, device_id_type=MESH,
        )

    def half_copy(t):
        return along(nb.at[pl.ds(0, HALF), rows_of(t)], half_in.at[:, rows_of(t)], half_send, half_recv, t, inner)

    def result(t):
        return nb.at[pl.ds(HALF, HALF), rows_of(t)]

    def out_half(t, which):
        return refined.at[pl.ds(which * HALF, HALF), rows_of(t)]

    def pair_copy(t):
        return along(result(t), out_half(t, mine), pair_send, pair_recv, t, inner)

    def next_copy(t):
        return along(result(t), out_half(t, mine), next_send, next_recv, t, outer)

    def near_copy(t):
        spot = refined.at[pl.ds((1 - mine) * HALF, NEAR), rows_of(t)]
        return along(spot, spot, near_send, near_recv, t, outer)

    def far_copy(t):
        spot = refined.at[pl.ds(mine * HALF + NEAR, HALF - NEAR), rows_of(t)]
        return along(spot, spot, far_send, far_recv, t, outer)

    def local_copy(t):
        return pltpu.make_async_copy(result(t), out_half(t, mine), local_sem.at[t])

    @pl.when(live)
    def _():
        def tick(t):
            @pl.when(t < CHUNKS)
            def _():
                def ahead(slot):
                    weight = kept[slot, :, rows_of(t), :].reshape(LINKS * CHUNK_ROWS, BLOCK)
                    sums = jnp.dot(weight, fetched[slot], preferred_element_type=jnp.float32)
                    forward[pl.ds(slot * LINKS, LINKS)] = (
                        sums.astype(jnp.bfloat16).reshape(LINKS, CHUNK_ROWS, FEATURES)
                    )

                each(SLOTS, ahead)

                @pl.when(t % WIDER == 0)
                def _():
                    each_slot(lambda slot: back_arrival(t // WIDER, slot).wait_recv())

                def piece(g):
                    rows = pl.ds(pl.multiple_of(g * PIECE, PIECE), PIECE)
                    spot = pl.ds(pl.multiple_of(t * CHUNK_ROWS + g * PIECE, PIECE), PIECE)
                    back_spot = pl.ds(pl.multiple_of((t % WIDER) * CHUNK_ROWS + g * PIECE, PIECE), PIECE)
                    terms = forward[:, rows, :].reshape(SLOTS * LINKS * PIECE, FEATURES)
                    came = returned[t // WIDER, :, back_spot, :].reshape(SLOTS * PIECE, FEATURES)
                    sums = jnp.dot(spread[...], terms, preferred_element_type=jnp.float32) + jnp.dot(
                        back_spread[...], came, preferred_element_type=jnp.float32
                    )
                    sums = sums.reshape(BLK_DEV, PIECE, FEATURES)
                    totals[:, spot, :] += sums[0:HALF]
                    nb[0:HALF, spot, :] = sums[HALF:BLK_DEV].astype(jnp.bfloat16)

                each(CHUNK_ROWS // PIECE, piece)
                half_copy(t).start()

            @pl.when(jnp.logical_and(t >= 1, t < CHUNKS + 1))
            def _():
                now = t - 1
                half_copy(now).wait_recv()

                def finish_block(k):
                    summed = totals[k, rows_of(now), :] + half_in[k, rows_of(now), :].astype(jnp.float32)
                    nb[HALF + k, rows_of(now), :] = row_scaled(summed).astype(jnp.bfloat16)

                each(HALF, finish_block)
                pair_copy(now).start()
                next_copy(now).start()
                local_copy(now).start()

            @pl.when(t >= 2)
            def _():
                pair_copy(t - 2).wait_recv()
                near_copy(t - 2).start()

        each(CHUNKS + 2, tick)

        def finish(t):
            half_copy(t).wait_send()
            pair_copy(t).wait_send()
            next_copy(t).wait_send()
            near_copy(t).wait_send()
            local_copy(t).wait()

        each(CHUNKS, finish)
        for t in range(BACKS):
            each_slot(lambda slot: back_copy(t, slot).wait_send())

    @pl.when(jnp.logical_not(live))
    def _():
        def tick(t):
            next_copy(t).wait_recv()
            far_copy(t).start()

        each(CHUNKS, tick)

        def finish(t):
            near_copy(t).wait_recv()
            far_copy(t).wait()

        each(CHUNKS, finish)

    each_sent(lambda slot: fetch_copy(slot).wait_send())


def on_device(embeddings, partner, links, counts):
    blocks = (BLK_DEV, BLOCK, FEATURES)
    smem = pl.BlockSpec(memory_space=pltpu.SMEM)
    dma = pltpu.SemaphoreType.DMA

    def vmem(*shape):
        return pltpu.VMEM(shape + (FEATURES,), jnp.bfloat16)

    refined = pl.pallas_call(
        whole_kernel,
        out_shape=jax.ShapeDtypeStruct(blocks, jnp.bfloat16),
        in_specs=[smem, smem, smem, pl.BlockSpec(memory_space=pl.ANY)],
        out_specs=pl.BlockSpec(memory_space=pl.ANY),
        scratch_shapes=[
            vmem(BLK_DEV, BLOCK),
            vmem(SLOTS, BLOCK),
            vmem(SLOTS, BLOCK),
            vmem(LINKS * BLOCK),
            pltpu.VMEM((SLOTS, LINKS, BLOCK, BLOCK), jnp.bfloat16),
            vmem(SLOTS * LINKS, CHUNK_ROWS),
            pltpu.VMEM((HALF, BLOCK, FEATURES), jnp.float32),
            vmem(SLOTS, BLOCK),
            pltpu.VMEM((BLK_DEV * PIECE, SLOTS * LINKS * PIECE), jnp.bfloat16),
            pltpu.VMEM((BLK_DEV * PIECE, SLOTS * PIECE), jnp.bfloat16),
            vmem(BACKS, SLOTS, BACK_ROWS),
            vmem(HALF, BLOCK),
            dma((BLK_DEV,)),
            dma((SLOTS,)),
            dma((SLOTS,)),
            dma((BACKS, SLOTS)),
            dma((BACKS, SLOTS)),
        ] + [dma((CHUNKS,))] * 11,
        compiler_params=pltpu.CompilerParams(
            collective_id=0, has_side_effects=True, vmem_limit_bytes=62 * 2**20
        ),
        name="whole",
    )(partner.reshape(-1), links.reshape(-1), counts.reshape(-1), embeddings.reshape(blocks))
    return refined.reshape(BLK_DEV * BLOCK, FEATURES)


def solution(mesh):
    placed = (P("rows", None), P(None, "rows"), P("rows", None, None), P("rows", None))
    return jax.shard_map(
        on_device, mesh=mesh, in_specs=placed, out_specs=P("rows", None), check_vma=False
    )
```

```python
import jax
import jax.numpy as jnp
from jax import lax
from jax.experimental import pallas as pl
from jax.experimental.pallas import tpu as pltpu
from jax.sharding import PartitionSpec as P

BLOCK = 256
FEATURES = 768
BLK_DEV = 16
HALF = BLK_DEV // 2
LINKS = 4
PLANES = 4
SLOTS = 16
CHUNKS = 8
CHUNK_ROWS = BLOCK // CHUNKS
BACKS = 4
BACK_ROWS = BLOCK // BACKS
WIDER = CHUNKS // BACKS
PIECE = 16
MESH = pl.DeviceIdType.MESH


def slot_at(turn):
    diagonal, step = turn // 4, turn % 4
    ties_first = jnp.where(step == 0, 2, jnp.where(step == 1, 1, jnp.where(step == 2, 3, 0)))
    step_x = jnp.where(diagonal <= 1, ties_first, jnp.where(diagonal == 2, step, (step + 2) % 4))
    return step_x * 4 + (step_x + diagonal) % 4


def live_core(parity, plane):
    upper = (plane + 4 - parity) % 2
    return ((plane + 8 - upper - parity) % 4) // 2


def idle_side(slot, upper):
    step_x, step_y = slot // 4, slot % 4
    return jnp.where((step_x + step_y) % 2 == 0, (step_x + upper + 1) % 2, 0)


def crossed(slot, idle):
    step_x, step_y = slot // 4, slot % 4
    return jnp.where(idle == 1, (step_x + 1 - 2 * (step_x % 2)) * 4 + step_y + 1 - 2 * (step_y % 2), slot)


def row_scaled(values):
    return values * lax.rsqrt(jnp.mean(values * values, axis=-1, keepdims=True) + 1e-06)


def cubed(cosines):
    weight = jnp.maximum(cosines * (1.0 / FEATURES), 0.0)
    return weight * weight * weight


def nt_dot(left, right):
    return lax.dot_general(left, right, (((1,), (1,)), ((), ())), preferred_element_type=jnp.float32)


def tn_dot(left, right):
    return lax.dot_general(left, right, (((0,), (0,)), ((), ())), preferred_element_type=jnp.float32)


def whole_kernel(wanted, links, counts, emb, refined, nb, out, fetched, cat, kept, forward, totals, back, spread,
                 back_spread, returned,
                 half_in, in_sem, fetch_send, fetch_recv, back_send, back_recv, half_send, half_recv, pair_send,
                 pair_recv, next_send, next_recv, near_send, near_recv, local_sem):
    me = lax.axis_index("rows")
    plane = lax.axis_index("grp")
    x, y, core = me // 8, (me // 2) % 4, me % 2
    parity = (x + y) % 2
    role = (plane + 4 - (2 * core + parity)) % 4
    live = role < 2
    upper = (plane + 4 - parity) % 2
    mine = jnp.where(jnp.logical_or(role == 1, role == 2), 1, 0)
    inner = (plane + 5 - 2 * mine) % PLANES
    outer = (plane + 3 + 2 * mine) % PLANES

    def each(count, action):
        def one(i, carry):
            action(i)
            return carry

        lax.fori_loop(0, count, one, 0)

    def each_slot(action):
        def one(turn):
            slot = slot_at(turn)

            @pl.when(not_self(slot))
            def _():
                action(slot)

        each(SLOTS, one)

    def not_self(slot):
        return jnp.logical_or(slot != 0, upper == 0)

    def chip(slot, sign):
        step_x, step_y = slot // 4, slot % 4
        there = ((x + sign * step_x + 4) % 4) * 8 + ((y + sign * step_y + 4) % 4) * 2
        return there, (parity + step_x + step_y) % 2

    def owner_of(slot):
        there, kind = chip(slot, -1)
        return there + (live_core(kind, plane) + idle_side(slot, upper)) % 2

    def owner_plane(slot):
        return (plane + 4 + idle_side(slot, upper) * (2 * upper - 1)) % PLANES

    def taker_of(slot):
        there, kind = chip(slot, 1)
        return there + live_core(kind, plane)

    def lister_of(slot):
        there, kind = chip(crossed(slot, idle_side(slot, upper)), 1)
        return there + live_core(kind, owner_plane(slot))

    def emb_copy(b):
        return pltpu.make_async_copy(emb.at[b], nb.at[b], in_sem.at[b])

    each(BLK_DEV, lambda b: emb_copy(b).start())
    barrier = pltpu.get_barrier_semaphore()

    @pl.when(live)
    def _():
        def greet(slot):
            pl.semaphore_signal(
                barrier, inc=1, device_id={"rows": owner_of(slot), "grp": plane}, device_id_type=MESH
            )
            pl.semaphore_signal(
                barrier, inc=1, device_id={"rows": lister_of(slot), "grp": owner_plane(slot)}, device_id_type=MESH
            )

        each_slot(greet)

    for side in (inner, outer):
        pl.semaphore_signal(barrier, inc=1, device_id={"rows": me, "grp": side}, device_id_type=MESH)

    each(BLK_DEV, lambda b: emb_copy(b).wait())
    pl.semaphore_wait(barrier, jnp.where(live, 30 - 2 * upper, 6))

    def fetch_copy(slot):
        return pltpu.make_async_remote_copy(
            src_ref=out.at[slot],
            dst_ref=fetched.at[slot],
            send_sem=fetch_send.at[slot],
            recv_sem=fetch_recv.at[slot],
            device_id={"rows": taker_of(slot), "grp": plane},
            device_id_type=MESH,
        )

    def each_sent(action):
        def one(slot):
            @pl.when(idle_side(slot, upper) == jnp.where(live, 0, 1))
            def _():
                action(slot)

        each_slot(one)

    def send(slot):
        out[slot] = row_scaled(nb[wanted[taker_of(slot)]].astype(jnp.float32)).astype(jnp.bfloat16)
        fetch_copy(slot).start()

    each_sent(send)

    def rows_of(t):
        return pl.ds(pl.multiple_of(t * CHUNK_ROWS, CHUNK_ROWS), CHUNK_ROWS)

    def back_rows(t):
        return pl.ds(pl.multiple_of(t * BACK_ROWS, BACK_ROWS), BACK_ROWS)

    def back_copy(t, slot):
        idle = idle_side(slot, upper)
        return pltpu.make_async_remote_copy(
            src_ref=back.at[slot, back_rows(t)],
            dst_ref=returned.at[t, crossed(slot, idle)],
            send_sem=back_send.at[t, slot],
            recv_sem=back_recv.at[t, crossed(slot, idle)],
            device_id={"rows": owner_of(slot), "grp": owner_plane(slot)},
            device_id_type=MESH,
        )

    def back_arrival(t, slot):
        return pltpu.make_async_remote_copy(
            src_ref=back.at[slot, back_rows(t)],
            dst_ref=returned.at[t, slot],
            send_sem=back_send.at[t, slot],
            recv_sem=back_recv.at[t, slot],
            device_id={"rows": lister_of(slot), "grp": owner_plane(slot)},
            device_id_type=MESH,
        )

    def one_hot(block_of, count):
        col = lax.broadcasted_iota(jnp.int32, (8, count * PIECE), 1)
        takes = jnp.zeros((8, count * PIECE), jnp.int32)
        for term in range(count):
            takes = jnp.where(col // PIECE == term, (block_of(term) + HALF * mine) % BLK_DEV, takes)
        row_id = lax.broadcasted_iota(jnp.int32, (BLK_DEV * PIECE, count * PIECE), 0)
        col_id = lax.broadcasted_iota(jnp.int32, (BLK_DEV * PIECE, count * PIECE), 1)
        return jnp.where(row_id == takes[0:1] * PIECE + col_id % PIECE, 1.0, 0.0).astype(jnp.bfloat16)

    @pl.when(live)
    def _():
        def normalise(b):
            nb[b] = row_scaled(nb[b].astype(jnp.float32)).astype(jnp.bfloat16)

        each(BLK_DEV, normalise)

        @pl.when(upper == 1)
        def _():
            fetched[0] = jnp.zeros((BLOCK, FEATURES), jnp.bfloat16)
            for t in range(BACKS):
                returned[t, 0] = jnp.zeros((BACK_ROWS, FEATURES), jnp.bfloat16)

        def diagonal(k):
            block = nb[mine * HALF + k]
            weight = cubed(nt_dot(block, block)).astype(jnp.bfloat16)
            totals[k] = jnp.dot(weight, block, preferred_element_type=jnp.float32)

        each(HALF, diagonal)
        back_spread[...] = one_hot(lambda term: wanted[lister_of(term)], SLOTS)
        spread[...] = one_hot(lambda term: links[term % LINKS, owner_of(term // LINKS)], SLOTS * LINKS)
        link_col = lax.broadcasted_iota(jnp.int32, (BLOCK, LINKS * BLOCK), 1)

        def visit(turn):
            slot = slot_at(turn)
            peer = owner_of(slot)

            @pl.when(not_self(slot))
            def _():
                fetch_copy(slot).wait_recv()

            for j in range(LINKS):
                cat[j * BLOCK:(j + 1) * BLOCK] = nb[links[j, peer]]
            weight = jnp.where(
                link_col < counts[peer] * BLOCK, cubed(nt_dot(fetched[slot], cat[...])), 0.0
            ).astype(jnp.bfloat16)
            back[slot] = jnp.dot(weight, cat[...], preferred_element_type=jnp.float32).astype(jnp.bfloat16)

            @pl.when(not_self(slot))
            def _():
                back_copy(0, slot).start()

            kept[slot] = weight.T.reshape(LINKS, BLOCK, BLOCK)

        each(SLOTS, visit)
        for t in range(1, BACKS):
            each_slot(lambda slot: back_copy(t, slot).start())

    def along(src, dst, send, recv, t, side):
        return pltpu.make_async_remote_copy(
            src_ref=src, dst_ref=dst, send_sem=send.at[t], recv_sem=recv.at[t],
            device_id={"rows": me, "grp": side}, device_id_type=MESH,
        )

    def half_copy(t):
        return along(nb.at[pl.ds(0, HALF), rows_of(t)], half_in.at[:, rows_of(t)], half_send, half_recv, t, inner)

    def result(t):
        return nb.at[pl.ds(HALF, HALF), rows_of(t)]

    def out_half(t, which):
        return refined.at[pl.ds(which * HALF, HALF), rows_of(t)]

    def pair_copy(t):
        return along(result(t), out_half(t, mine), pair_send, pair_recv, t, inner)

    def next_copy(t):
        return along(result(t), out_half(t, mine), next_send, next_recv, t, outer)

    def near_copy(t):
        spot = out_half(t, 1 - mine)
        return along(spot, spot, near_send, near_recv, t, outer)

    def local_copy(t):
        return pltpu.make_async_copy(result(t), out_half(t, mine), local_sem.at[t])

    @pl.when(live)
    def _():
        def tick(t):
            @pl.when(t < CHUNKS)
            def _():
                def ahead(slot):
                    weight = kept[slot, :, rows_of(t), :].reshape(LINKS * CHUNK_ROWS, BLOCK)
                    sums = jnp.dot(weight, fetched[slot], preferred_element_type=jnp.float32)
                    forward[pl.ds(slot * LINKS, LINKS)] = (
                        sums.astype(jnp.bfloat16).reshape(LINKS, CHUNK_ROWS, FEATURES)
                    )

                each(SLOTS, ahead)

                @pl.when(t % WIDER == 0)
                def _():
                    each_slot(lambda slot: back_arrival(t // WIDER, slot).wait_recv())

                def piece(g):
                    rows = pl.ds(pl.multiple_of(g * PIECE, PIECE), PIECE)
                    spot = pl.ds(pl.multiple_of(t * CHUNK_ROWS + g * PIECE, PIECE), PIECE)
                    back_spot = pl.ds(pl.multiple_of((t % WIDER) * CHUNK_ROWS + g * PIECE, PIECE), PIECE)
                    terms = forward[:, rows, :].reshape(SLOTS * LINKS * PIECE, FEATURES)
                    came = returned[t // WIDER, :, back_spot, :].reshape(SLOTS * PIECE, FEATURES)
                    sums = jnp.dot(spread[...], terms, preferred_element_type=jnp.float32) + jnp.dot(
                        back_spread[...], came, preferred_element_type=jnp.float32
                    )
                    sums = sums.reshape(BLK_DEV, PIECE, FEATURES)
                    totals[:, spot, :] += sums[0:HALF]
                    nb[0:HALF, spot, :] = sums[HALF:BLK_DEV].astype(jnp.bfloat16)

                each(CHUNK_ROWS // PIECE, piece)
                half_copy(t).start()

            @pl.when(jnp.logical_and(t >= 1, t < CHUNKS + 1))
            def _():
                now = t - 1
                half_copy(now).wait_recv()

                def finish_block(k):
                    summed = totals[k, rows_of(now), :] + half_in[k, rows_of(now), :].astype(jnp.float32)
                    nb[HALF + k, rows_of(now), :] = row_scaled(summed).astype(jnp.bfloat16)

                each(HALF, finish_block)
                pair_copy(now).start()
                next_copy(now).start()
                local_copy(now).start()

            @pl.when(t >= 2)
            def _():
                pair_copy(t - 2).wait_recv()
                near_copy(t - 2).start()

        each(CHUNKS + 2, tick)

        def finish(t):
            half_copy(t).wait_send()
            pair_copy(t).wait_send()
            next_copy(t).wait_send()
            near_copy(t).wait_send()
            local_copy(t).wait()

        each(CHUNKS, finish)
        for t in range(BACKS):
            each_slot(lambda slot: back_copy(t, slot).wait_send())

    @pl.when(jnp.logical_not(live))
    def _():
        def tick(t):
            next_copy(t).wait_recv()

        each(CHUNKS, tick)

        def finish(t):
            near_copy(t).wait_recv()

        each(CHUNKS, finish)

    each_sent(lambda slot: fetch_copy(slot).wait_send())


def on_device(embeddings, partner, links, counts):
    blocks = (BLK_DEV, BLOCK, FEATURES)
    smem = pl.BlockSpec(memory_space=pltpu.SMEM)
    dma = pltpu.SemaphoreType.DMA

    def vmem(*shape):
        return pltpu.VMEM(shape + (FEATURES,), jnp.bfloat16)

    refined = pl.pallas_call(
        whole_kernel,
        out_shape=jax.ShapeDtypeStruct(blocks, jnp.bfloat16),
        in_specs=[smem, smem, smem, pl.BlockSpec(memory_space=pl.ANY)],
        out_specs=pl.BlockSpec(memory_space=pl.ANY),
        scratch_shapes=[
            vmem(BLK_DEV, BLOCK),
            vmem(SLOTS, BLOCK),
            vmem(SLOTS, BLOCK),
            vmem(LINKS * BLOCK),
            pltpu.VMEM((SLOTS, LINKS, BLOCK, BLOCK), jnp.bfloat16),
            vmem(SLOTS * LINKS, CHUNK_ROWS),
            pltpu.VMEM((HALF, BLOCK, FEATURES), jnp.float32),
            vmem(SLOTS, BLOCK),
            pltpu.VMEM((BLK_DEV * PIECE, SLOTS * LINKS * PIECE), jnp.bfloat16),
            pltpu.VMEM((BLK_DEV * PIECE, SLOTS * PIECE), jnp.bfloat16),
            vmem(BACKS, SLOTS, BACK_ROWS),
            vmem(HALF, BLOCK),
            dma((BLK_DEV,)),
            dma((SLOTS,)),
            dma((SLOTS,)),
            dma((BACKS, SLOTS)),
            dma((BACKS, SLOTS)),
        ] + [dma((CHUNKS,))] * 9,
        compiler_params=pltpu.CompilerParams(
            collective_id=0, has_side_effects=True, vmem_limit_bytes=62 * 2**20
        ),
        name="whole",
    )(partner.reshape(-1), links[0].T, counts.reshape(-1), embeddings.reshape(blocks))
    return refined.reshape(BLK_DEV * BLOCK, FEATURES)


def solution(mesh):
    placed = (P("rows", None), P(None, "rows"), P("rows", None, None), P("rows", None))
    return jax.shard_map(
        on_device, mesh=mesh, in_specs=placed, out_specs=P("rows", None), check_vma=False
    )
```

```python
import jax
import jax.numpy as jnp
from jax import lax
from jax.experimental import pallas as pl
from jax.experimental.pallas import tpu as pltpu
from jax.sharding import PartitionSpec as P

BLOCK = 256
FEATURES = 768
BLK_DEV = 16
HALF = BLK_DEV // 2
LINKS = 4
PLANES = 4
SLOTS = 16
CHUNKS = 8
CHUNK_ROWS = BLOCK // CHUNKS
BACKS = 4
BACK_ROWS = BLOCK // BACKS
WIDER = CHUNKS // BACKS
PIECE = 16
MESH = pl.DeviceIdType.MESH


def slot_at(turn):
    diagonal, step = turn // 4, turn % 4
    ties_first = jnp.where(step == 0, 2, jnp.where(step == 1, 1, jnp.where(step == 2, 3, 0)))
    step_x = jnp.where(diagonal <= 1, ties_first, jnp.where(diagonal == 2, step, (step + 2) % 4))
    return step_x * 4 + (step_x + diagonal) % 4


def live_core(parity, plane):
    upper = (plane + 4 - parity) % 2
    return ((plane + 8 - upper - parity) % 4) // 2


def idle_side(slot, upper):
    step_x, step_y = slot // 4, slot % 4
    return jnp.where((step_x + step_y) % 2 == 0, (step_x + upper + 1) % 2, 0)


def crossed(slot, idle):
    step_x, step_y = slot // 4, slot % 4
    return jnp.where(idle == 1, (step_x + 1 - 2 * (step_x % 2)) * 4 + step_y + 1 - 2 * (step_y % 2), slot)


def row_scaled(values):
    return values * lax.rsqrt(jnp.mean(values * values, axis=-1, keepdims=True) + 1e-06)


def cubed(cosines):
    weight = jnp.maximum(cosines * (1.0 / FEATURES), 0.0)
    return weight * weight * weight


def nt_dot(left, right):
    return lax.dot_general(left, right, (((1,), (1,)), ((), ())), preferred_element_type=jnp.float32)


def tn_dot(left, right):
    return lax.dot_general(left, right, (((0,), (0,)), ((), ())), preferred_element_type=jnp.float32)


def whole_kernel(wanted, links, counts, emb, refined, nb, out, fetched, cat, kept, forward, totals, back, spread,
                 back_spread, returned,
                 half_in, in_sem, fetch_send, fetch_recv, back_send, back_recv, half_send, half_recv, pair_send,
                 pair_recv, next_send, next_recv, near_send, near_recv, local_sem):
    me = lax.axis_index("rows")
    plane = lax.axis_index("grp")
    x, y, core = me // 8, (me // 2) % 4, me % 2
    parity = (x + y) % 2
    role = (plane + 4 - (2 * core + parity)) % 4
    live = role < 2
    upper = (plane + 4 - parity) % 2
    mine = jnp.where(jnp.logical_or(role == 1, role == 2), 1, 0)
    inner = (plane + 5 - 2 * mine) % PLANES
    outer = (plane + 3 + 2 * mine) % PLANES

    def each(count, action):
        def one(i, carry):
            action(i)
            return carry

        lax.fori_loop(0, count, one, 0)

    def each_slot(action):
        def one(turn):
            slot = slot_at(turn)

            @pl.when(not_self(slot))
            def _():
                action(slot)

        each(SLOTS, one)

    def not_self(slot):
        return jnp.logical_or(slot != 0, upper == 0)

    def chip(slot, sign):
        step_x, step_y = slot // 4, slot % 4
        there = ((x + sign * step_x + 4) % 4) * 8 + ((y + sign * step_y + 4) % 4) * 2
        return there, (parity + step_x + step_y) % 2

    def owner_of(slot):
        there, kind = chip(slot, -1)
        return there + (live_core(kind, plane) + idle_side(slot, upper)) % 2

    def owner_plane(slot):
        return (plane + 4 + idle_side(slot, upper) * (2 * upper - 1)) % PLANES

    def taker_of(slot):
        there, kind = chip(slot, 1)
        return there + live_core(kind, plane)

    def lister_of(slot):
        there, kind = chip(crossed(slot, idle_side(slot, upper)), 1)
        return there + live_core(kind, owner_plane(slot))

    def emb_copy(b):
        return pltpu.make_async_copy(emb.at[b], nb.at[b], in_sem.at[b])

    each(BLK_DEV, lambda b: emb_copy(b).start())
    barrier = pltpu.get_barrier_semaphore()

    @pl.when(live)
    def _():
        def greet(slot):
            pl.semaphore_signal(
                barrier, inc=1, device_id={"rows": owner_of(slot), "grp": plane}, device_id_type=MESH
            )
            pl.semaphore_signal(
                barrier, inc=1, device_id={"rows": lister_of(slot), "grp": owner_plane(slot)}, device_id_type=MESH
            )

        each_slot(greet)

    for side in (inner, outer):
        pl.semaphore_signal(barrier, inc=1, device_id={"rows": me, "grp": side}, device_id_type=MESH)

    each(BLK_DEV, lambda b: emb_copy(b).wait())
    pl.semaphore_wait(barrier, jnp.where(live, 30 - 2 * upper, 6))

    def fetch_copy(slot):
        return pltpu.make_async_remote_copy(
            src_ref=out.at[slot],
            dst_ref=fetched.at[slot],
            send_sem=fetch_send.at[slot],
            recv_sem=fetch_recv.at[slot],
            device_id={"rows": taker_of(slot), "grp": plane},
            device_id_type=MESH,
        )

    def each_sent(action):
        def one(slot):
            @pl.when(idle_side(slot, upper) == jnp.where(live, 0, 1))
            def _():
                action(slot)

        each_slot(one)

    def send(slot):
        out[slot] = row_scaled(nb[wanted[taker_of(slot)]].astype(jnp.float32)).astype(jnp.bfloat16)
        fetch_copy(slot).start()

    each_sent(send)

    def rows_of(t):
        return pl.ds(pl.multiple_of(t * CHUNK_ROWS, CHUNK_ROWS), CHUNK_ROWS)

    def back_rows(t):
        return pl.ds(pl.multiple_of(t * BACK_ROWS, BACK_ROWS), BACK_ROWS)

    def back_copy(t, slot):
        idle = idle_side(slot, upper)
        return pltpu.make_async_remote_copy(
            src_ref=back.at[slot, back_rows(t)],
            dst_ref=returned.at[t, crossed(slot, idle)],
            send_sem=back_send.at[t, slot],
            recv_sem=back_recv.at[t, crossed(slot, idle)],
            device_id={"rows": owner_of(slot), "grp": owner_plane(slot)},
            device_id_type=MESH,
        )

    def back_arrival(t, slot):
        return pltpu.make_async_remote_copy(
            src_ref=back.at[slot, back_rows(t)],
            dst_ref=returned.at[t, slot],
            send_sem=back_send.at[t, slot],
            recv_sem=back_recv.at[t, slot],
            device_id={"rows": lister_of(slot), "grp": owner_plane(slot)},
            device_id_type=MESH,
        )

    def one_hot(block_of, count):
        col = lax.broadcasted_iota(jnp.int32, (8, count * PIECE), 1)
        takes = jnp.zeros((8, count * PIECE), jnp.int32)
        for term in range(count):
            takes = jnp.where(col // PIECE == term, (block_of(term) + HALF * mine) % BLK_DEV, takes)
        row_id = lax.broadcasted_iota(jnp.int32, (BLK_DEV * PIECE, count * PIECE), 0)
        col_id = lax.broadcasted_iota(jnp.int32, (BLK_DEV * PIECE, count * PIECE), 1)
        return jnp.where(row_id == takes[0:1] * PIECE + col_id % PIECE, 1.0, 0.0).astype(jnp.bfloat16)

    @pl.when(live)
    def _():
        def normalise(b):
            nb[b] = row_scaled(nb[b].astype(jnp.float32)).astype(jnp.bfloat16)

        each(BLK_DEV, normalise)

        @pl.when(upper == 1)
        def _():
            fetched[0] = jnp.zeros((BLOCK, FEATURES), jnp.bfloat16)
            for t in range(BACKS):
                returned[t, 0] = jnp.zeros((BACK_ROWS, FEATURES), jnp.bfloat16)

        def diagonal(k):
            block = nb[mine * HALF + k]
            weight = cubed(nt_dot(block, block)).astype(jnp.bfloat16)
            totals[k] = jnp.dot(weight, block, preferred_element_type=jnp.float32)

        each(HALF, diagonal)
        back_spread[...] = one_hot(lambda term: wanted[lister_of(term)], SLOTS)
        spread[...] = one_hot(lambda term: links[term % LINKS, owner_of(term // LINKS)], SLOTS * LINKS)
        link_col = lax.broadcasted_iota(jnp.int32, (BLOCK, LINKS * BLOCK), 1)

        def visit(turn):
            slot = slot_at(turn)
            peer = owner_of(slot)

            @pl.when(not_self(slot))
            def _():
                fetch_copy(slot).wait_recv()

            for j in range(LINKS):
                cat[j * BLOCK:(j + 1) * BLOCK] = nb[links[j, peer]]
            weight = jnp.where(
                link_col < counts[peer] * BLOCK, cubed(nt_dot(fetched[slot], cat[...])), 0.0
            ).astype(jnp.bfloat16)
            back[slot] = jnp.dot(weight, cat[...], preferred_element_type=jnp.float32).astype(jnp.bfloat16)

            @pl.when(not_self(slot))
            def _():
                back_copy(0, slot).start()

            kept[slot] = weight.T.reshape(LINKS, BLOCK, BLOCK)

        each(SLOTS, visit)
        def send_rest(t, slot, idle):
            @pl.when(idle_side(slot, upper) == idle)
            def _():
                back_copy(t, slot).start()

        for t in range(1, BACKS):
            for idle in (1, 0):
                each_slot(lambda slot: send_rest(t, slot, idle))

    def along(src, dst, send, recv, t, side):
        return pltpu.make_async_remote_copy(
            src_ref=src, dst_ref=dst, send_sem=send.at[t], recv_sem=recv.at[t],
            device_id={"rows": me, "grp": side}, device_id_type=MESH,
        )

    def half_copy(t):
        return along(nb.at[pl.ds(0, HALF), rows_of(t)], half_in.at[:, rows_of(t)], half_send, half_recv, t, inner)

    def result(t):
        return nb.at[pl.ds(HALF, HALF), rows_of(t)]

    def out_half(t, which):
        return refined.at[pl.ds(which * HALF, HALF), rows_of(t)]

    def pair_copy(t):
        return along(result(t), out_half(t, mine), pair_send, pair_recv, t, inner)

    def next_copy(t):
        return along(result(t), out_half(t, mine), next_send, next_recv, t, outer)

    def near_copy(t):
        spot = out_half(t, 1 - mine)
        return along(spot, spot, near_send, near_recv, t, outer)

    def local_copy(t):
        return pltpu.make_async_copy(result(t), out_half(t, mine), local_sem.at[t])

    @pl.when(live)
    def _():
        def tick(t):
            @pl.when(t < CHUNKS)
            def _():
                def ahead(slot):
                    weight = kept[slot, :, rows_of(t), :].reshape(LINKS * CHUNK_ROWS, BLOCK)
                    sums = jnp.dot(weight, fetched[slot], preferred_element_type=jnp.float32)
                    forward[pl.ds(slot * LINKS, LINKS)] = (
                        sums.astype(jnp.bfloat16).reshape(LINKS, CHUNK_ROWS, FEATURES)
                    )

                each(SLOTS, ahead)

                @pl.when(t % WIDER == 0)
                def _():
                    each_slot(lambda slot: back_arrival(t // WIDER, slot).wait_recv())

                def piece(g):
                    rows = pl.ds(pl.multiple_of(g * PIECE, PIECE), PIECE)
                    spot = pl.ds(pl.multiple_of(t * CHUNK_ROWS + g * PIECE, PIECE), PIECE)
                    back_spot = pl.ds(pl.multiple_of((t % WIDER) * CHUNK_ROWS + g * PIECE, PIECE), PIECE)
                    terms = forward[:, rows, :].reshape(SLOTS * LINKS * PIECE, FEATURES)
                    came = returned[t // WIDER, :, back_spot, :].reshape(SLOTS * PIECE, FEATURES)
                    sums = jnp.dot(spread[...], terms, preferred_element_type=jnp.float32) + jnp.dot(
                        back_spread[...], came, preferred_element_type=jnp.float32
                    )
                    sums = sums.reshape(BLK_DEV, PIECE, FEATURES)
                    totals[:, spot, :] += sums[0:HALF]
                    nb[0:HALF, spot, :] = sums[HALF:BLK_DEV].astype(jnp.bfloat16)

                each(CHUNK_ROWS // PIECE, piece)
                half_copy(t).start()

            @pl.when(jnp.logical_and(t >= 1, t < CHUNKS + 1))
            def _():
                now = t - 1
                half_copy(now).wait_recv()

                def finish_block(k):
                    summed = totals[k, rows_of(now), :] + half_in[k, rows_of(now), :].astype(jnp.float32)
                    nb[HALF + k, rows_of(now), :] = row_scaled(summed).astype(jnp.bfloat16)

                each(HALF, finish_block)
                pair_copy(now).start()
                next_copy(now).start()
                local_copy(now).start()

            @pl.when(t >= 2)
            def _():
                pair_copy(t - 2).wait_recv()
                near_copy(t - 2).start()

        each(CHUNKS + 2, tick)

        def finish(t):
            half_copy(t).wait_send()
            pair_copy(t).wait_send()
            next_copy(t).wait_send()
            near_copy(t).wait_send()
            local_copy(t).wait()

        each(CHUNKS, finish)
        for t in range(BACKS):
            each_slot(lambda slot: back_copy(t, slot).wait_send())

    @pl.when(jnp.logical_not(live))
    def _():
        def tick(t):
            next_copy(t).wait_recv()

        each(CHUNKS, tick)

        def finish(t):
            near_copy(t).wait_recv()

        each(CHUNKS, finish)

    each_sent(lambda slot: fetch_copy(slot).wait_send())


def on_device(embeddings, partner, links, counts):
    blocks = (BLK_DEV, BLOCK, FEATURES)
    smem = pl.BlockSpec(memory_space=pltpu.SMEM)
    dma = pltpu.SemaphoreType.DMA

    def vmem(*shape):
        return pltpu.VMEM(shape + (FEATURES,), jnp.bfloat16)

    refined = pl.pallas_call(
        whole_kernel,
        out_shape=jax.ShapeDtypeStruct(blocks, jnp.bfloat16),
        in_specs=[smem, smem, smem, pl.BlockSpec(memory_space=pl.ANY)],
        out_specs=pl.BlockSpec(memory_space=pl.ANY),
        scratch_shapes=[
            vmem(BLK_DEV, BLOCK),
            vmem(SLOTS, BLOCK),
            vmem(SLOTS, BLOCK),
            vmem(LINKS * BLOCK),
            pltpu.VMEM((SLOTS, LINKS, BLOCK, BLOCK), jnp.bfloat16),
            vmem(SLOTS * LINKS, CHUNK_ROWS),
            pltpu.VMEM((HALF, BLOCK, FEATURES), jnp.float32),
            vmem(SLOTS, BLOCK),
            pltpu.VMEM((BLK_DEV * PIECE, SLOTS * LINKS * PIECE), jnp.bfloat16),
            pltpu.VMEM((BLK_DEV * PIECE, SLOTS * PIECE), jnp.bfloat16),
            vmem(BACKS, SLOTS, BACK_ROWS),
            vmem(HALF, BLOCK),
            dma((BLK_DEV,)),
            dma((SLOTS,)),
            dma((SLOTS,)),
            dma((BACKS, SLOTS)),
            dma((BACKS, SLOTS)),
        ] + [dma((CHUNKS,))] * 9,
        compiler_params=pltpu.CompilerParams(
            collective_id=0, has_side_effects=True, vmem_limit_bytes=62 * 2**20
        ),
        name="whole",
    )(partner.reshape(-1), links[0].T, counts.reshape(-1), embeddings.reshape(blocks))
    return refined.reshape(BLK_DEV * BLOCK, FEATURES)


def solution(mesh):
    placed = (P("rows", None), P(None, "rows"), P("rows", None, None), P("rows", None))
    return jax.shard_map(
        on_device, mesh=mesh, in_specs=placed, out_specs=P("rows", None), check_vma=False
    )
```

```python
import jax
import jax.numpy as jnp
from jax import lax
from jax.experimental import pallas as pl
from jax.experimental.pallas import tpu as pltpu
from jax.sharding import PartitionSpec as P

BLOCK = 256
FEATURES = 768
BLK_DEV = 16
HALF = BLK_DEV // 2
LINKS = 4
PLANES = 4
SLOTS = 16
CHUNKS = 8
CHUNK_ROWS = BLOCK // CHUNKS
BACKS = 4
BACK_ROWS = BLOCK // BACKS
WIDER = CHUNKS // BACKS
PIECE = 16
MESH = pl.DeviceIdType.MESH


def slot_at(turn):
    diagonal, step = turn // 4, turn % 4
    ties_first = jnp.where(step == 0, 2, jnp.where(step == 1, 1, jnp.where(step == 2, 3, 0)))
    step_x = jnp.where(diagonal <= 1, ties_first, jnp.where(diagonal == 2, step, (step + 2) % 4))
    return step_x * 4 + (step_x + diagonal) % 4


def live_core(parity, plane):
    upper = (plane + 4 - parity) % 2
    return ((plane + 8 - upper - parity) % 4) // 2


def idle_side(slot, upper):
    step_x, step_y = slot // 4, slot % 4
    return jnp.where((step_x + step_y) % 2 == 0, (step_x + upper + 1) % 2, 0)


def crossed(slot, idle):
    step_x, step_y = slot // 4, slot % 4
    return jnp.where(idle == 1, (step_x + 1 - 2 * (step_x % 2)) * 4 + step_y + 1 - 2 * (step_y % 2), slot)


def row_scaled(values):
    return values * lax.rsqrt(jnp.mean(values * values, axis=-1, keepdims=True) + 1e-06)


def cubed(cosines):
    weight = jnp.maximum(cosines * (1.0 / FEATURES), 0.0)
    return weight * weight * weight


def nt_dot(left, right):
    return lax.dot_general(left, right, (((1,), (1,)), ((), ())), preferred_element_type=jnp.float32)


def tn_dot(left, right):
    return lax.dot_general(left, right, (((0,), (0,)), ((), ())), preferred_element_type=jnp.float32)


def whole_kernel(wanted, links, counts, emb, refined, nb, out, fetched, cat, kept, forward, totals, back, spread,
                 back_spread, returned,
                 half_in, in_sem, fetch_send, fetch_recv, back_send, back_recv, half_send, half_recv, pair_send,
                 pair_recv, next_send, next_recv, near_send, near_recv, local_sem):
    me = lax.axis_index("rows")
    plane = lax.axis_index("grp")
    x, y, core = me // 8, (me // 2) % 4, me % 2
    parity = (x + y) % 2
    role = (plane + 4 - (2 * core + parity)) % 4
    live = role < 2
    upper = (plane + 4 - parity) % 2
    mine = jnp.where(jnp.logical_or(role == 1, role == 2), 1, 0)
    inner = (plane + 5 - 2 * mine) % PLANES
    outer = (plane + 3 + 2 * mine) % PLANES

    def each(count, action):
        def one(i, carry):
            action(i)
            return carry

        lax.fori_loop(0, count, one, 0)

    def each_slot(action):
        def one(turn):
            slot = slot_at(turn)

            @pl.when(not_self(slot))
            def _():
                action(slot)

        each(SLOTS, one)

    def not_self(slot):
        return jnp.logical_or(slot != 0, upper == 0)

    def chip(slot, sign):
        step_x, step_y = slot // 4, slot % 4
        there = ((x + sign * step_x + 4) % 4) * 8 + ((y + sign * step_y + 4) % 4) * 2
        return there, (parity + step_x + step_y) % 2

    def owner_of(slot):
        there, kind = chip(slot, -1)
        return there + (live_core(kind, plane) + idle_side(slot, upper)) % 2

    def owner_plane(slot):
        return (plane + 4 + idle_side(slot, upper) * (2 * upper - 1)) % PLANES

    def taker_of(slot):
        there, kind = chip(slot, 1)
        return there + live_core(kind, plane)

    def lister_of(slot):
        there, kind = chip(crossed(slot, idle_side(slot, upper)), 1)
        return there + live_core(kind, owner_plane(slot))

    def emb_copy(b):
        return pltpu.make_async_copy(emb.at[b], nb.at[b], in_sem.at[b])

    each(BLK_DEV, lambda b: emb_copy(b).start())
    barrier = pltpu.get_barrier_semaphore()

    @pl.when(live)
    def _():
        def greet(slot):
            pl.semaphore_signal(
                barrier, inc=1, device_id={"rows": owner_of(slot), "grp": plane}, device_id_type=MESH
            )
            pl.semaphore_signal(
                barrier, inc=1, device_id={"rows": lister_of(slot), "grp": owner_plane(slot)}, device_id_type=MESH
            )

        each_slot(greet)

    for side in (inner, outer):
        pl.semaphore_signal(barrier, inc=1, device_id={"rows": me, "grp": side}, device_id_type=MESH)

    each(BLK_DEV, lambda b: emb_copy(b).wait())
    pl.semaphore_wait(barrier, jnp.where(live, 30 - 2 * upper, 6))

    def fetch_copy(slot):
        return pltpu.make_async_remote_copy(
            src_ref=out.at[slot],
            dst_ref=fetched.at[slot],
            send_sem=fetch_send.at[slot],
            recv_sem=fetch_recv.at[slot],
            device_id={"rows": taker_of(slot), "grp": plane},
            device_id_type=MESH,
        )

    def each_sent(action):
        def one(slot):
            @pl.when(idle_side(slot, upper) == jnp.where(live, 0, 1))
            def _():
                action(slot)

        each_slot(one)

    def send(slot):
        out[slot] = row_scaled(nb[wanted[taker_of(slot)]].astype(jnp.float32)).astype(jnp.bfloat16)
        fetch_copy(slot).start()

    each_sent(send)

    def rows_of(t):
        return pl.ds(pl.multiple_of(t * CHUNK_ROWS, CHUNK_ROWS), CHUNK_ROWS)

    def back_rows(t):
        return pl.ds(pl.multiple_of(t * BACK_ROWS, BACK_ROWS), BACK_ROWS)

    def back_copy(t, slot):
        idle = idle_side(slot, upper)
        return pltpu.make_async_remote_copy(
            src_ref=back.at[slot, back_rows(t)],
            dst_ref=returned.at[t, crossed(slot, idle)],
            send_sem=back_send.at[t, slot],
            recv_sem=back_recv.at[t, crossed(slot, idle)],
            device_id={"rows": owner_of(slot), "grp": owner_plane(slot)},
            device_id_type=MESH,
        )

    def back_arrival(t, slot):
        return pltpu.make_async_remote_copy(
            src_ref=back.at[slot, back_rows(t)],
            dst_ref=returned.at[t, slot],
            send_sem=back_send.at[t, slot],
            recv_sem=back_recv.at[t, slot],
            device_id={"rows": lister_of(slot), "grp": owner_plane(slot)},
            device_id_type=MESH,
        )

    def one_hot(block_of, count):
        col = lax.broadcasted_iota(jnp.int32, (8, count * PIECE), 1)
        takes = jnp.zeros((8, count * PIECE), jnp.int32)
        for term in range(count):
            takes = jnp.where(col // PIECE == term, (block_of(term) + HALF * mine) % BLK_DEV, takes)
        row_id = lax.broadcasted_iota(jnp.int32, (BLK_DEV * PIECE, count * PIECE), 0)
        col_id = lax.broadcasted_iota(jnp.int32, (BLK_DEV * PIECE, count * PIECE), 1)
        return jnp.where(row_id == takes[0:1] * PIECE + col_id % PIECE, 1.0, 0.0).astype(jnp.bfloat16)

    @pl.when(live)
    def _():
        def normalise(b):
            nb[b] = row_scaled(nb[b].astype(jnp.float32)).astype(jnp.bfloat16)

        each(BLK_DEV, normalise)

        @pl.when(upper == 1)
        def _():
            fetched[0] = jnp.zeros((BLOCK, FEATURES), jnp.bfloat16)
            for t in range(BACKS):
                returned[t, 0] = jnp.zeros((BACK_ROWS, FEATURES), jnp.bfloat16)

        def diagonal(k):
            block = nb[mine * HALF + k]
            weight = cubed(nt_dot(block, block)).astype(jnp.bfloat16)
            totals[k] = jnp.dot(weight, block, preferred_element_type=jnp.float32)

        each(HALF, diagonal)
        back_spread[...] = one_hot(lambda term: wanted[lister_of(term)], SLOTS)
        spread[...] = one_hot(lambda term: links[term % LINKS, owner_of(term // LINKS)], SLOTS * LINKS)
        link_col = lax.broadcasted_iota(jnp.int32, (BLOCK, LINKS * BLOCK), 1)

        def visit(turn):
            slot = slot_at(turn)
            peer = owner_of(slot)

            @pl.when(not_self(slot))
            def _():
                fetch_copy(slot).wait_recv()

            for j in range(LINKS):
                cat[j * BLOCK:(j + 1) * BLOCK] = nb[links[j, peer]]
            weight = jnp.where(
                link_col < counts[peer] * BLOCK, cubed(nt_dot(fetched[slot], cat[...])), 0.0
            ).astype(jnp.bfloat16)
            back[slot] = jnp.dot(weight, cat[...], preferred_element_type=jnp.float32).astype(jnp.bfloat16)

            @pl.when(not_self(slot))
            def _():
                back_copy(0, slot).start()

            kept[slot] = weight.T.reshape(LINKS, BLOCK, BLOCK)

        each(SLOTS, visit)
        def send_rest(t, slot, idle):
            @pl.when(idle_side(slot, upper) == idle)
            def _():
                back_copy(t, slot).start()

        for t in range(1, BACKS):
            for idle in (1, 0):
                each_slot(lambda slot: send_rest(t, slot, idle))

    def along(src, dst, send, recv, t, side):
        return pltpu.make_async_remote_copy(
            src_ref=src, dst_ref=dst, send_sem=send.at[t], recv_sem=recv.at[t],
            device_id={"rows": me, "grp": side}, device_id_type=MESH,
        )

    def half_copy(t):
        return along(nb.at[pl.ds(0, HALF), rows_of(t)], half_in.at[:, rows_of(t)], half_send, half_recv, t, inner)

    def result(t):
        return nb.at[pl.ds(HALF, HALF), rows_of(t)]

    def out_half(t, which):
        return refined.at[pl.ds(which * HALF, HALF), rows_of(t)]

    def pair_copy(t):
        return along(result(t), out_half(t, mine), pair_send, pair_recv, t, inner)

    def next_copy(t):
        return along(result(t), out_half(t, mine), next_send, next_recv, t, outer)

    def near_copy(t):
        spot = out_half(t, 1 - mine)
        return along(spot, spot, near_send, near_recv, t, outer)

    def local_copy(t):
        return pltpu.make_async_copy(result(t), out_half(t, mine), local_sem.at[t])

    @pl.when(live)
    def _():
        def forward_sums(t):
            def one(slot):
                weight = kept[slot, :, rows_of(t), :].reshape(LINKS * CHUNK_ROWS, BLOCK)
                sums = jnp.dot(weight, fetched[slot], preferred_element_type=jnp.float32)
                forward[pl.ds(slot * LINKS, LINKS)] = sums.astype(jnp.bfloat16).reshape(LINKS, CHUNK_ROWS, FEATURES)

            each(SLOTS, one)

        forward_sums(0)

        def tick(t):
            @pl.when(t < CHUNKS)
            def _():
                @pl.when(t % WIDER == 0)
                def _():
                    each_slot(lambda slot: back_arrival(t // WIDER, slot).wait_recv())

                def piece(g):
                    rows = pl.ds(pl.multiple_of(g * PIECE, PIECE), PIECE)
                    spot = pl.ds(pl.multiple_of(t * CHUNK_ROWS + g * PIECE, PIECE), PIECE)
                    back_spot = pl.ds(pl.multiple_of((t % WIDER) * CHUNK_ROWS + g * PIECE, PIECE), PIECE)
                    terms = forward[:, rows, :].reshape(SLOTS * LINKS * PIECE, FEATURES)
                    came = returned[t // WIDER, :, back_spot, :].reshape(SLOTS * PIECE, FEATURES)
                    sums = jnp.dot(spread[...], terms, preferred_element_type=jnp.float32) + jnp.dot(
                        back_spread[...], came, preferred_element_type=jnp.float32
                    )
                    sums = sums.reshape(BLK_DEV, PIECE, FEATURES)
                    totals[:, spot, :] += sums[0:HALF]
                    nb[0:HALF, spot, :] = sums[HALF:BLK_DEV].astype(jnp.bfloat16)

                each(CHUNK_ROWS // PIECE, piece)
                half_copy(t).start()

            @pl.when(jnp.logical_and(t >= 1, t < CHUNKS + 1))
            def _():
                now = t - 1
                half_copy(now).wait_recv()

                def finish_block(k):
                    summed = totals[k, rows_of(now), :] + half_in[k, rows_of(now), :].astype(jnp.float32)
                    nb[HALF + k, rows_of(now), :] = row_scaled(summed).astype(jnp.bfloat16)

                each(HALF, finish_block)
                pair_copy(now).start()
                next_copy(now).start()
                local_copy(now).start()

            @pl.when(t >= 2)
            def _():
                pair_copy(t - 2).wait_recv()
                near_copy(t - 2).start()

            @pl.when(t + 1 < CHUNKS)
            def _():
                forward_sums(t + 1)

        each(CHUNKS + 2, tick)

        def finish(t):
            half_copy(t).wait_send()
            pair_copy(t).wait_send()
            next_copy(t).wait_send()
            near_copy(t).wait_send()
            local_copy(t).wait()

        each(CHUNKS, finish)
        for t in range(BACKS):
            each_slot(lambda slot: back_copy(t, slot).wait_send())

    @pl.when(jnp.logical_not(live))
    def _():
        def tick(t):
            next_copy(t).wait_recv()

        each(CHUNKS, tick)

        def finish(t):
            near_copy(t).wait_recv()

        each(CHUNKS, finish)

    each_sent(lambda slot: fetch_copy(slot).wait_send())


def on_device(embeddings, partner, links, counts):
    blocks = (BLK_DEV, BLOCK, FEATURES)
    smem = pl.BlockSpec(memory_space=pltpu.SMEM)
    dma = pltpu.SemaphoreType.DMA

    def vmem(*shape):
        return pltpu.VMEM(shape + (FEATURES,), jnp.bfloat16)

    refined = pl.pallas_call(
        whole_kernel,
        out_shape=pltpu.VMEM(blocks, jnp.bfloat16),
        in_specs=[smem, smem, smem, pl.BlockSpec(memory_space=pl.ANY)],
        out_specs=pl.BlockSpec(memory_space=pl.ANY),
        scratch_shapes=[
            vmem(BLK_DEV, BLOCK),
            vmem(SLOTS, BLOCK),
            vmem(SLOTS, BLOCK),
            vmem(LINKS * BLOCK),
            pltpu.VMEM((SLOTS, LINKS, BLOCK, BLOCK), jnp.bfloat16),
            vmem(SLOTS * LINKS, CHUNK_ROWS),
            pltpu.VMEM((HALF, BLOCK, FEATURES), jnp.float32),
            vmem(SLOTS, BLOCK),
            pltpu.VMEM((BLK_DEV * PIECE, SLOTS * LINKS * PIECE), jnp.bfloat16),
            pltpu.VMEM((BLK_DEV * PIECE, SLOTS * PIECE), jnp.bfloat16),
            vmem(BACKS, SLOTS, BACK_ROWS),
            vmem(HALF, BLOCK),
            dma((BLK_DEV,)),
            dma((SLOTS,)),
            dma((SLOTS,)),
            dma((BACKS, SLOTS)),
            dma((BACKS, SLOTS)),
        ] + [dma((CHUNKS,))] * 9,
        compiler_params=pltpu.CompilerParams(
            collective_id=0, has_side_effects=True, vmem_limit_bytes=56 * 2**20
        ),
        name="whole",
    )(partner.reshape(-1), links[0].T, counts.reshape(-1), embeddings.reshape(blocks))
    return refined.reshape(BLK_DEV * BLOCK, FEATURES)


def solution(mesh):
    placed = (P("rows", None), P(None, "rows"), P("rows", None, None), P("rows", None))
    return jax.shard_map(
        on_device, mesh=mesh, in_specs=placed, out_specs=P("rows", None), check_vma=False
    )
```

```python
import jax
import jax.numpy as jnp
from jax import lax
from jax.experimental import pallas as pl
from jax.experimental.pallas import tpu as pltpu
from jax.sharding import PartitionSpec as P

BLOCK = 256
FEATURES = 768
BLK_DEV = 16
HALF = BLK_DEV // 2
LINKS = 4
PLANES = 4
SLOTS = 16
CHUNKS = 8
CHUNK_ROWS = BLOCK // CHUNKS
BACKS = 4
BACK_ROWS = BLOCK // BACKS
WIDER = CHUNKS // BACKS
PIECE = 16
MESH = pl.DeviceIdType.MESH


def slot_at(turn):
    diagonal, step = turn // 4, turn % 4
    ties_first = jnp.where(step == 0, 2, jnp.where(step == 1, 1, jnp.where(step == 2, 3, 0)))
    step_x = jnp.where(diagonal <= 1, ties_first, jnp.where(diagonal == 2, step, (step + 2) % 4))
    return step_x * 4 + (step_x + diagonal) % 4


def live_core(parity, plane):
    upper = (plane + 4 - parity) % 2
    return ((plane + 8 - upper - parity) % 4) // 2


def idle_side(slot, upper):
    step_x, step_y = slot // 4, slot % 4
    return jnp.where((step_x + step_y) % 2 == 0, (step_x + upper + 1) % 2, 0)


def crossed(slot, idle):
    step_x, step_y = slot // 4, slot % 4
    return jnp.where(idle == 1, (step_x + 1 - 2 * (step_x % 2)) * 4 + step_y + 1 - 2 * (step_y % 2), slot)


def row_scaled(values):
    return values * lax.rsqrt(jnp.mean(values * values, axis=-1, keepdims=True) + 1e-06)


def cubed(cosines):
    weight = jnp.maximum(cosines * (1.0 / FEATURES), 0.0)
    return weight * weight * weight


def nt_dot(left, right):
    return lax.dot_general(left, right, (((1,), (1,)), ((), ())), preferred_element_type=jnp.float32)


def tn_dot(left, right):
    return lax.dot_general(left, right, (((0,), (0,)), ((), ())), preferred_element_type=jnp.float32)


def whole_kernel(wanted, links, counts, emb, refined, nb, out, fetched, cat, kept, forward, totals, back, spread,
                 back_spread, returned,
                 half_in, in_sem, fetch_send, fetch_recv, back_send, back_recv, half_send, half_recv, pair_send,
                 pair_recv, next_send, next_recv, near_send, near_recv):
    me = lax.axis_index("rows")
    plane = lax.axis_index("grp")
    x, y, core = me // 8, (me // 2) % 4, me % 2
    parity = (x + y) % 2
    role = (plane + 4 - (2 * core + parity)) % 4
    live = role < 2
    upper = (plane + 4 - parity) % 2
    mine = jnp.where(jnp.logical_or(role == 1, role == 2), 1, 0)
    inner = (plane + 5 - 2 * mine) % PLANES
    outer = (plane + 3 + 2 * mine) % PLANES

    def each(count, action):
        def one(i, carry):
            action(i)
            return carry

        lax.fori_loop(0, count, one, 0)

    def each_slot(action):
        def one(turn):
            slot = slot_at(turn)

            @pl.when(not_self(slot))
            def _():
                action(slot)

        each(SLOTS, one)

    def not_self(slot):
        return jnp.logical_or(slot != 0, upper == 0)

    def chip(slot, sign):
        step_x, step_y = slot // 4, slot % 4
        there = ((x + sign * step_x + 4) % 4) * 8 + ((y + sign * step_y + 4) % 4) * 2
        return there, (parity + step_x + step_y) % 2

    def owner_of(slot):
        there, kind = chip(slot, -1)
        return there + (live_core(kind, plane) + idle_side(slot, upper)) % 2

    def owner_plane(slot):
        return (plane + 4 + idle_side(slot, upper) * (2 * upper - 1)) % PLANES

    def taker_of(slot):
        there, kind = chip(slot, 1)
        return there + live_core(kind, plane)

    def lister_of(slot):
        there, kind = chip(crossed(slot, idle_side(slot, upper)), 1)
        return there + live_core(kind, owner_plane(slot))

    def emb_copy(b):
        return pltpu.make_async_copy(emb.at[b], nb.at[b], in_sem.at[b])

    each(BLK_DEV, lambda b: emb_copy(b).start())
    barrier = pltpu.get_barrier_semaphore()

    @pl.when(live)
    def _():
        def greet(slot):
            pl.semaphore_signal(
                barrier, inc=1, device_id={"rows": owner_of(slot), "grp": plane}, device_id_type=MESH
            )
            pl.semaphore_signal(
                barrier, inc=1, device_id={"rows": lister_of(slot), "grp": owner_plane(slot)}, device_id_type=MESH
            )

        each_slot(greet)

    for side in (inner, outer):
        pl.semaphore_signal(barrier, inc=1, device_id={"rows": me, "grp": side}, device_id_type=MESH)

    each(BLK_DEV, lambda b: emb_copy(b).wait())
    pl.semaphore_wait(barrier, jnp.where(live, 30 - 2 * upper, 6))

    def fetch_copy(slot):
        return pltpu.make_async_remote_copy(
            src_ref=out.at[slot],
            dst_ref=fetched.at[slot],
            send_sem=fetch_send.at[slot],
            recv_sem=fetch_recv.at[slot],
            device_id={"rows": taker_of(slot), "grp": plane},
            device_id_type=MESH,
        )

    def each_sent(action):
        def one(slot):
            @pl.when(idle_side(slot, upper) == jnp.where(live, 0, 1))
            def _():
                action(slot)

        each_slot(one)

    def send(slot):
        out[slot] = row_scaled(nb[wanted[taker_of(slot)]].astype(jnp.float32)).astype(jnp.bfloat16)
        fetch_copy(slot).start()

    each_sent(send)

    def rows_of(t):
        return pl.ds(pl.multiple_of(t * CHUNK_ROWS, CHUNK_ROWS), CHUNK_ROWS)

    def back_rows(t):
        return pl.ds(pl.multiple_of(t * BACK_ROWS, BACK_ROWS), BACK_ROWS)

    def back_copy(t, slot):
        idle = idle_side(slot, upper)
        return pltpu.make_async_remote_copy(
            src_ref=back.at[slot, back_rows(t)],
            dst_ref=returned.at[t, crossed(slot, idle)],
            send_sem=back_send.at[t, slot],
            recv_sem=back_recv.at[t, crossed(slot, idle)],
            device_id={"rows": owner_of(slot), "grp": owner_plane(slot)},
            device_id_type=MESH,
        )

    def back_arrival(t, slot):
        return pltpu.make_async_remote_copy(
            src_ref=back.at[slot, back_rows(t)],
            dst_ref=returned.at[t, slot],
            send_sem=back_send.at[t, slot],
            recv_sem=back_recv.at[t, slot],
            device_id={"rows": lister_of(slot), "grp": owner_plane(slot)},
            device_id_type=MESH,
        )

    def one_hot(block_of, count):
        col = lax.broadcasted_iota(jnp.int32, (8, count * PIECE), 1)
        takes = jnp.zeros((8, count * PIECE), jnp.int32)
        for term in range(count):
            takes = jnp.where(col // PIECE == term, (block_of(term) + HALF * mine) % BLK_DEV, takes)
        row_id = lax.broadcasted_iota(jnp.int32, (BLK_DEV * PIECE, count * PIECE), 0)
        col_id = lax.broadcasted_iota(jnp.int32, (BLK_DEV * PIECE, count * PIECE), 1)
        return jnp.where(row_id == takes[0:1] * PIECE + col_id % PIECE, 1.0, 0.0).astype(jnp.bfloat16)

    @pl.when(live)
    def _():
        def normalise(b):
            nb[b] = row_scaled(nb[b].astype(jnp.float32)).astype(jnp.bfloat16)

        each(BLK_DEV, normalise)

        @pl.when(upper == 1)
        def _():
            fetched[0] = jnp.zeros((BLOCK, FEATURES), jnp.bfloat16)
            for t in range(BACKS):
                returned[t, 0] = jnp.zeros((BACK_ROWS, FEATURES), jnp.bfloat16)

        def diagonal(k):
            block = nb[mine * HALF + k]
            weight = cubed(nt_dot(block, block)).astype(jnp.bfloat16)
            totals[k] = jnp.dot(weight, block, preferred_element_type=jnp.float32)

        each(HALF, diagonal)
        back_spread[...] = one_hot(lambda term: wanted[lister_of(term)], SLOTS)
        spread[...] = one_hot(lambda term: links[term % LINKS, owner_of(term // LINKS)], SLOTS * LINKS)
        link_col = lax.broadcasted_iota(jnp.int32, (BLOCK, LINKS * BLOCK), 1)

        def visit(turn):
            slot = slot_at(turn)
            peer = owner_of(slot)

            @pl.when(not_self(slot))
            def _():
                fetch_copy(slot).wait_recv()

            for j in range(LINKS):
                cat[j * BLOCK:(j + 1) * BLOCK] = nb[links[j, peer]]
            weight = jnp.where(
                link_col < counts[peer] * BLOCK, cubed(nt_dot(fetched[slot], cat[...])), 0.0
            ).astype(jnp.bfloat16)
            back[slot] = jnp.dot(weight, cat[...], preferred_element_type=jnp.float32).astype(jnp.bfloat16)

            @pl.when(not_self(slot))
            def _():
                back_copy(0, slot).start()

            kept[slot] = weight.T.reshape(LINKS, BLOCK, BLOCK)

        each(SLOTS, visit)
        def send_rest(t, slot, idle):
            @pl.when(idle_side(slot, upper) == idle)
            def _():
                back_copy(t, slot).start()

        for t in range(1, BACKS):
            for idle in (1, 0):
                each_slot(lambda slot: send_rest(t, slot, idle))

    def along(src, dst, send, recv, t, side):
        return pltpu.make_async_remote_copy(
            src_ref=src, dst_ref=dst, send_sem=send.at[t], recv_sem=recv.at[t],
            device_id={"rows": me, "grp": side}, device_id_type=MESH,
        )

    def half_copy(t):
        return along(nb.at[pl.ds(0, HALF), rows_of(t)], half_in.at[:, rows_of(t)], half_send, half_recv, t, inner)

    def out_half(t, which):
        return refined.at[pl.ds(which * HALF, HALF), rows_of(t)]

    def pair_copy(t):
        return along(out_half(t, mine), out_half(t, mine), pair_send, pair_recv, t, inner)

    def next_copy(t):
        return along(out_half(t, mine), out_half(t, mine), next_send, next_recv, t, outer)

    def near_copy(t):
        spot = out_half(t, 1 - mine)
        return along(spot, spot, near_send, near_recv, t, outer)

    @pl.when(live)
    def _():
        def forward_sums(t):
            def one(slot):
                weight = kept[slot, :, rows_of(t), :].reshape(LINKS * CHUNK_ROWS, BLOCK)
                sums = jnp.dot(weight, fetched[slot], preferred_element_type=jnp.float32)
                forward[pl.ds(slot * LINKS, LINKS)] = sums.astype(jnp.bfloat16).reshape(LINKS, CHUNK_ROWS, FEATURES)

            each(SLOTS, one)

        forward_sums(0)

        def tick(t):
            @pl.when(t < CHUNKS)
            def _():
                @pl.when(t % WIDER == 0)
                def _():
                    each_slot(lambda slot: back_arrival(t // WIDER, slot).wait_recv())

                def piece(g):
                    rows = pl.ds(pl.multiple_of(g * PIECE, PIECE), PIECE)
                    spot = pl.ds(pl.multiple_of(t * CHUNK_ROWS + g * PIECE, PIECE), PIECE)
                    back_spot = pl.ds(pl.multiple_of((t % WIDER) * CHUNK_ROWS + g * PIECE, PIECE), PIECE)
                    terms = forward[:, rows, :].reshape(SLOTS * LINKS * PIECE, FEATURES)
                    came = returned[t // WIDER, :, back_spot, :].reshape(SLOTS * PIECE, FEATURES)
                    sums = jnp.dot(spread[...], terms, preferred_element_type=jnp.float32) + jnp.dot(
                        back_spread[...], came, preferred_element_type=jnp.float32
                    )
                    sums = sums.reshape(BLK_DEV, PIECE, FEATURES)
                    totals[:, spot, :] += sums[0:HALF]
                    nb[0:HALF, spot, :] = sums[HALF:BLK_DEV].astype(jnp.bfloat16)

                each(CHUNK_ROWS // PIECE, piece)
                half_copy(t).start()

            @pl.when(jnp.logical_and(t >= 1, t < CHUNKS + 1))
            def _():
                now = t - 1
                half_copy(now).wait_recv()

                def finish_block(k):
                    summed = totals[k, rows_of(now), :] + half_in[k, rows_of(now), :].astype(jnp.float32)
                    refined[mine * HALF + k, rows_of(now), :] = row_scaled(summed).astype(jnp.bfloat16)

                each(HALF, finish_block)
                pair_copy(now).start()
                next_copy(now).start()

            @pl.when(t >= 2)
            def _():
                pair_copy(t - 2).wait_recv()
                near_copy(t - 2).start()

            @pl.when(t + 1 < CHUNKS)
            def _():
                forward_sums(t + 1)

        each(CHUNKS + 2, tick)

        def finish(t):
            half_copy(t).wait_send()
            pair_copy(t).wait_send()
            next_copy(t).wait_send()
            near_copy(t).wait_send()

        each(CHUNKS, finish)
        for t in range(BACKS):
            each_slot(lambda slot: back_copy(t, slot).wait_send())

    @pl.when(jnp.logical_not(live))
    def _():
        def tick(t):
            next_copy(t).wait_recv()

        each(CHUNKS, tick)

        def finish(t):
            near_copy(t).wait_recv()

        each(CHUNKS, finish)

    each_sent(lambda slot: fetch_copy(slot).wait_send())


def on_device(embeddings, partner, links, counts):
    blocks = (BLK_DEV, BLOCK, FEATURES)
    smem = pl.BlockSpec(memory_space=pltpu.SMEM)
    dma = pltpu.SemaphoreType.DMA

    def vmem(*shape):
        return pltpu.VMEM(shape + (FEATURES,), jnp.bfloat16)

    refined = pl.pallas_call(
        whole_kernel,
        out_shape=pltpu.VMEM(blocks, jnp.bfloat16),
        in_specs=[smem, smem, smem, pl.BlockSpec(memory_space=pl.ANY)],
        out_specs=pl.BlockSpec(memory_space=pltpu.VMEM),
        scratch_shapes=[
            vmem(BLK_DEV, BLOCK),
            vmem(SLOTS, BLOCK),
            vmem(SLOTS, BLOCK),
            vmem(LINKS * BLOCK),
            pltpu.VMEM((SLOTS, LINKS, BLOCK, BLOCK), jnp.bfloat16),
            vmem(SLOTS * LINKS, CHUNK_ROWS),
            pltpu.VMEM((HALF, BLOCK, FEATURES), jnp.float32),
            vmem(SLOTS, BLOCK),
            pltpu.VMEM((BLK_DEV * PIECE, SLOTS * LINKS * PIECE), jnp.bfloat16),
            pltpu.VMEM((BLK_DEV * PIECE, SLOTS * PIECE), jnp.bfloat16),
            vmem(BACKS, SLOTS, BACK_ROWS),
            vmem(HALF, BLOCK),
            dma((BLK_DEV,)),
            dma((SLOTS,)),
            dma((SLOTS,)),
            dma((BACKS, SLOTS)),
            dma((BACKS, SLOTS)),
        ] + [dma((CHUNKS,))] * 8,
        compiler_params=pltpu.CompilerParams(
            collective_id=0, has_side_effects=True, vmem_limit_bytes=56 * 2**20
        ),
        name="whole",
    )(partner.reshape(-1), links[0].T, counts.reshape(-1), embeddings.reshape(blocks))
    return refined.reshape(BLK_DEV * BLOCK, FEATURES)


def solution(mesh):
    placed = (P("rows", None), P(None, "rows"), P("rows", None, None), P("rows", None))
    return jax.shard_map(
        on_device, mesh=mesh, in_specs=placed, out_specs=P("rows", None), check_vma=False
    )
```
